128 devices in a mesh: coil: 8 (over y, core), space: 16 (over z, x).
Axes of the slice: x: 4, y: 4, z: 4, core: 2. Of those that a mesh axis runs over, the one named last changes fastest.
Arguments:
- image: float32 [2, 8, 512, 512], P(None, None, 'space'), may hold values from -6 to 6
- residual: float32 [2, 8, 512, 512], P(None, None, 'space'), may hold values from -20 to 20
- direction: float32 [2, 8, 512, 512], P(None, None, 'space'), may hold values from -20 to 20
- sensitivity: bfloat16 [2, 32, 8, 512, 512], P(None, 'coil', None, 'space'), may hold values from -1.2 to 1.2
- sampling: int32 [512, 512], P(None, 'space'), may hold values from 0 to 1
Outputs:
- image_next: float32 [2, 8, 512, 512], P(None, None, 'space', 'coil')
- residual_next: float32 [2, 8, 512, 512], P(None, None, 'space', 'coil')
- direction_next: float32 [2, 8, 512, 512], P(None, None, 'space', 'coil')
The draws below stay inside these ranges and needn't reach their ends.
All inputs are finite; a program needn't handle non-finite values.
Results may differ from the reference program's by a relative error of at most 0.0019.
Values may be sent and summed in bfloat16 or wider, within the bound.
No kernel may reach another device: no remote copies, remote signals or barrier semaphores. Data moves between devices by JAX's collectives and lax.ppermute only.
A program may use at most 128 MiB of HBM per device.

```python
import math
import jax
import jax.numpy as jnp
from jax import lax

NY = 512
NZ = 512
X = 8
COILS = 32


def smooth_modes(key, lead_shape, count, amplitude):
    top_freq = max(1, NY // 128)
    z_turns = jnp.arange(NZ, dtype=jnp.float32) * (2.0 * math.pi / NZ)
    y_turns = jnp.arange(NY, dtype=jnp.float32) * (2.0 * math.pi / NY)
    summed = jnp.zeros(lead_shape + (NZ, NY), jnp.float32)
    for term_index in range(count):
        key_term = jax.random.fold_in(key, term_index)
        key_depth, key_across, key_phase, key_scale = jax.random.split(key_term, 4)
        freq_depth = jax.random.randint(key_depth, lead_shape, 0, top_freq + 1).astype(jnp.float32)
        freq_across = jax.random.randint(key_across, lead_shape, -top_freq, top_freq + 1).astype(jnp.float32)
        offset_phase = jax.random.uniform(key_phase, lead_shape, jnp.float32, -math.pi, math.pi)
        term_weight = jax.random.normal(key_scale, lead_shape, jnp.float32) * amplitude
        argument = freq_depth[..., None, None] * z_turns[:, None] + freq_across[..., None, None] * y_turns[None, :] + offset_phase[..., None, None]
        summed = summed + term_weight[..., None, None] * jnp.cos(argument)
    return summed


def normal_field(key, growth, spread):
    key_cells, key_rows, key_modes = jax.random.split(key, 3)
    samples = jnp.clip(jax.random.normal(key_cells, (2, X, NZ, NY), jnp.float32), -5.0, 5.0)
    across = jax.random.uniform(key_rows, (NY,), jnp.float32, -spread, spread)
    z_depth = jnp.arange(NZ, dtype=jnp.float32) / NZ
    rising = jnp.exp(z_depth * math.log(growth))
    rough = samples * jnp.exp(across)[None, None, None, :] * 0.6
    smooth = smooth_modes(key_modes, (2, X), 4, 0.7)
    return jnp.clip((rough + smooth) * rising[None, None, :, None], -20.0, 20.0)


def draw_residual(key, part):
    key = jax.random.fold_in(key, 11)
    return normal_field(key, 3.0, 0.5)


def draw_direction(key, part):
    key = jax.random.fold_in(key, 23)
    return normal_field(key, 3.0, 0.5)


def draw_sensitivity(key, part):
    key = jax.random.fold_in(key, 37)
    key_noise, key_modes = jax.random.split(key)
    smooth = smooth_modes(key_modes, (2, COILS, X), 4, 0.25)
    rough = jnp.clip(jax.random.normal(key_noise, (2, COILS, X, NZ, NY), jnp.float32) * 0.1, -0.5, 0.5)
    return jnp.clip(smooth + rough, -1.1875, 1.1875).astype(jnp.bfloat16)


def draw_sampling(key, part):
    key = jax.random.fold_in(key, 53)
    picked = jax.random.randint(key, (NZ, NY), 0, 3) == 0
    depth_index = jnp.arange(NZ, dtype=jnp.int32)
    across_index = jnp.arange(NY, dtype=jnp.int32)
    near_depth = jnp.minimum(depth_index, NZ - depth_index) < NZ // 16
    near_across = jnp.minimum(across_index, NY - across_index) < NY // 16
    centre_block = near_depth[:, None] & near_across[None, :]
    return (picked | centre_block).astype(jnp.int32)


def shard_levels(rng, shape, cuts, smallest, largest):
    gain, own = 1.0, jax.random.fold_in(rng, 6)
    for axis_at, parts in cuts:
        draws = jnp.exp(jax.random.uniform(jax.random.fold_in(own, axis_at), (parts,), jnp.float32, smallest / len(cuts), largest / len(cuts)))
        gain = gain * jnp.repeat(draws, shape[axis_at] // parts).reshape([-1 if axis == axis_at else 1 for axis in range(len(shape))])
    return gain


def scatter_about(rng, shape, scale, reach, cuts=(), kind=jnp.bfloat16):
    array = scale * jax.random.normal(rng, shape, jnp.float32)
    if cuts:
        array = array * shard_levels(rng, shape, cuts, -0.22, 0.18)
    return jnp.clip(array, -reach, reach).astype(kind)


def setup_inputs(seed: int = 0) -> dict:
    keys = jax.random.split(jax.random.key(seed), 6)
    image = scatter_about(keys[0], (2, X, NZ, NY), 1.0, 6.0, ((2, 16),), jnp.float32)
    residual = draw_residual(jax.random.fold_in(keys[5], 71), 0)
    direction = draw_direction(jax.random.fold_in(keys[5], 71), 0)
    sensitivity = draw_sensitivity(jax.random.fold_in(keys[5], 71), 0)
    sampling = draw_sampling(jax.random.fold_in(keys[5], 71), 0)
    return dict(image=image, residual=residual, direction=direction, sensitivity=sensitivity, sampling=sampling)


ridge_weight = 0.1

def tables(length):
    counter = jnp.arange(length, dtype=jnp.int32)
    product_mod = counter[:, None] * counter[None, :] % length
    phase_angle = product_mod.astype(jnp.float32) * (2.0 * math.pi / length)
    norm_scale = 1.0 / math.sqrt(length)
    return ((jnp.cos(phase_angle) * norm_scale).astype(jnp.bfloat16), (jnp.sin(phase_angle) * norm_scale).astype(jnp.bfloat16))

def transform(pattern, real_part, imag_part, cos_t, sin_t, orient):
    cos_f = cos_t.astype(jnp.float32)
    sin_f = sin_t.astype(jnp.float32)
    real_f = real_part.astype(jnp.float32)
    imag_f = imag_part.astype(jnp.float32)
    high = lax.Precision.HIGHEST
    real_cos = jnp.einsum(pattern, real_f, cos_f, precision=high)
    real_sin = jnp.einsum(pattern, real_f, sin_f, precision=high)
    imag_cos = jnp.einsum(pattern, imag_f, cos_f, precision=high)
    imag_sin = jnp.einsum(pattern, imag_f, sin_f, precision=high)
    return (real_cos + orient * imag_sin, imag_cos - orient * real_sin)

def reference(image, residual, direction, sensitivity, sampling):
    cos_y, sin_y = tables(NY)
    cos_z, sin_z = tables(NZ)
    keep_mask = sampling.astype(jnp.float32)
    dir_re = direction[0]
    dir_im = direction[1]

    def one_coil(running, slices):
        sens_re = slices[0].astype(jnp.float32)
        sens_im = slices[1].astype(jnp.float32)
        coil_re = (sens_re * dir_re - sens_im * dir_im).astype(jnp.bfloat16)
        coil_im = (sens_re * dir_im + sens_im * dir_re).astype(jnp.bfloat16)
        spec_re, spec_im = transform('xzn,nk->xzk', coil_re, coil_im, cos_y, sin_y, 1.0)
        spec_re = spec_re.astype(jnp.bfloat16)
        spec_im = spec_im.astype(jnp.bfloat16)
        kz_re, kz_im = transform('xny,nk->xky', spec_re, spec_im, cos_z, sin_z, 1.0)
        kept_re = (kz_re * keep_mask).astype(jnp.bfloat16)
        kept_im = (kz_im * keep_mask).astype(jnp.bfloat16)
        back_re, back_im = transform('xky,kn->xny', kept_re, kept_im, cos_z, sin_z, -1.0)
        back_re = back_re.astype(jnp.bfloat16)
        back_im = back_im.astype(jnp.bfloat16)
        field_re, field_im = transform('xzk,kn->xzn', back_re, back_im, cos_y, sin_y, -1.0)
        summed_re = sens_re * field_re + sens_im * field_im
        summed_im = sens_re * field_im - sens_im * field_re
        return ((running[0] + summed_re, running[1] + summed_im), None)
    zeros = jnp.zeros(dir_re.shape, jnp.float32)
    totals, unused = lax.scan(one_coil, (zeros, zeros), (sensitivity[0], sensitivity[1]))
    applied = jnp.stack(totals) + ridge_weight * direction
    old_norm = jnp.sum(residual * residual)
    curvature = jnp.sum(direction * applied)
    step_len = old_norm / curvature
    image_next = image + step_len * direction
    residual_next = residual - step_len * applied
    new_norm = jnp.sum(residual_next * residual_next)
    direction_next = residual_next + new_norm / old_norm * direction
    return (image_next, residual_next, direction_next)
```

```python
import math

import jax
import jax.numpy as jnp
import ml_dtypes
import numpy as np
from jax import lax
from jax.experimental import pallas as pl
from jax.experimental.pallas import tpu as pltpu
from jax.sharding import PartitionSpec as P

ridge_weight = 0.1
vmem_limit = 8 * 1024 * 1024


def tables(length):
    counter = np.arange(length, dtype=np.int32)
    product_mod = counter[:, None] * counter[None, :] % length
    phase_angle = product_mod.astype(np.float32) * np.float32(2.0 * math.pi / length)
    norm_scale = np.float32(1.0 / math.sqrt(length))
    return np.cos(phase_angle) * norm_scale, np.sin(phase_angle) * norm_scale


def fold_tables(length):
    cos_t, sin_t = tables(length)
    half = length // 2
    even, odd = np.arange(0, half, 2), np.arange(1, half, 2)
    low = np.concatenate([even, odd])
    high = np.where(low == 0, half, length - low)
    sine = sin_t[:, low].copy()
    sine[:, 0] = cos_t[:, half]
    fold = np.concatenate([cos_t[:, low], sine], axis=1)
    order = np.concatenate([low, high])
    pick = np.eye(length, dtype=np.float32)[:, order]
    outs = [fold, fold.T, pick, pick.T]
    for group in (even, odd):
        at = np.concatenate([group, np.where(group == 0, half, length - group)])
        cos_g, sin_g = cos_t[:half, at], sin_t[:half, at]
        block = np.block([[cos_g, -sin_g], [sin_g, cos_g]])
        outs += [block, block.T]
    return [np.ascontiguousarray(out).astype(ml_dtypes.bfloat16) for out in outs]


def pack_kernel(core_ref, sens_ref, dir_ref, mask_ref, out_ref, dir_s, mask_s, sems):
    core_rows = pl.ds(pl.multiple_of(core_ref[0] * 16, 16), 16)
    small = [
        pltpu.make_async_copy(dir_ref.at[:, :, core_rows, :], dir_s, sems.at[8]),
        pltpu.make_async_copy(mask_ref.at[core_rows, :], mask_s, sems.at[9]),
    ]
    large = [
        pltpu.make_async_copy(
            sens_ref.at[part, half * 2 + pick],
            out_ref.at[:, half, pl.ds((part * 2 + pick) * 32, 32), :],
            sems.at[pick * 4 + part * 2 + half],
        )
        for pick in range(2)
        for part in range(2)
        for half in range(2)
    ]
    for copy in small + large:
        copy.start()
    for copy in small:
        copy.wait()
    kept = mask_s[...].astype(jnp.bfloat16)
    for x in range(8):
        for half in range(2):
            for part in range(2):
                out_ref[x, half, pl.ds(128 + part * 16, 16), :] = dir_s[part, x].astype(jnp.bfloat16)
            out_ref[x, half, pl.ds(160, 16), :] = kept
    for copy in large:
        copy.wait()


def pack(core, sensitivity, direction, mask_t):
    hbm = pl.BlockSpec(memory_space=pltpu.HBM)
    return pl.pallas_call(
        pack_kernel,
        in_specs=[pl.BlockSpec(memory_space=pltpu.SMEM), hbm, hbm, hbm],
        out_specs=pl.BlockSpec(memory_space=pltpu.VMEM),
        out_shape=jax.ShapeDtypeStruct((8, 2, 176, 512), jnp.bfloat16),
        scratch_shapes=[
            pltpu.VMEM((2, 8, 16, 512), jnp.float32),
            pltpu.VMEM((16, 512), jnp.int32),
            pltpu.SemaphoreType.DMA((10,)),
        ],
        compiler_params=pltpu.CompilerParams(vmem_limit_bytes=60 * 1024 * 1024),
        name="pack",
    )(core, sensitivity, direction, mask_t)


def operator_kernel(
    coil_ref, got_ref, mate_ref, fold_ref, fold_t_ref, pick_ref, pick_t_ref,
    z_even_ref, y_even_ref, z_odd_ref, y_odd_ref, dir_ref, res_ref, img_ref,
    keep_ref, send_ref, own_ref,
    image_s, spec_s, even_s, odd_s, rows_s, mask_s, own_s, sems,
):
    size = 512
    half = 256
    f32 = jnp.float32
    bf16 = jnp.bfloat16
    core = coil_ref[0] % 2
    own_lanes = pl.ds(pl.multiple_of(coil_ref[0] // 2 * 128, 128), 128)
    own_copies = [
        pltpu.make_async_copy(ref.at[:, :, :, own_lanes], own_s.at[index], sems.at[index])
        for index, ref in enumerate((dir_ref, res_ref, img_ref))
    ]
    for copy in own_copies:
        copy.start()

    def dot(left, right):
        return jnp.dot(left, right, preferred_element_type=f32)

    for kind in range(3):
        rows_s[kind, :, core] = got_ref[:, pl.ds(128 + kind * 16, 16), :]
        rows_s[kind, :, 1 - core] = mate_ref[:, pl.ds(kind * 16, 16), :]

    mask_t = dot(pick_t_ref[...], rows_s[2].reshape(size, size)).astype(bf16)
    mask_s[...] = dot(mask_t, pick_ref[...]).T

    def sens(coil, part, block, lanes):
        rows = got_ref[pl.ds(block * 8, 8), pl.ds((part * 2 + coil) * 32, 32), lanes]
        return rows.reshape(half, -1).astype(f32)

    first_lane = lax.broadcasted_iota(jnp.int32, (half, 128), 1) == 0
    for coil in range(2):
        for block in range(2):
            rows = pl.ds(block * half, half)
            for yb in range(2):
                cols = pl.ds(yb * half, half)
                dir_re, dir_im = (
                    rows_s[part, pl.ds(block * 8, 8), :, :, cols].reshape(half, half).astype(f32) for part in range(2)
                )
                sens_re, sens_im = (sens(coil, part, block, cols) for part in range(2))
                image_s[coil, 0, rows, cols] = (sens_re * dir_re - sens_im * dir_im).astype(bf16)
                image_s[coil, 1, rows, cols] = (sens_re * dir_im + sens_im * dir_re).astype(bf16)
            from_re = dot(image_s[coil, 0, rows, :], fold_ref[...])
            from_im = dot(image_s[coil, 1, rows, :], fold_ref[...])
            re_cos, re_sin = from_re[:, :half], from_re[:, half:]
            im_cos, im_sin = from_im[:, :half], from_im[:, half:]
            low = (re_cos + im_sin, im_cos - re_sin)
            high = (re_cos - im_sin, im_cos + re_sin)
            low_first = (re_cos, im_cos)
            high_first = (re_sin, im_sin)
            for part in range(2):
                for start, value, first in ((0, low[part], low_first[part]), (half, high[part], high_first[part])):
                    spec_s[coil, part, rows, pl.ds(start, 128)] = jnp.where(
                        first_lane, first[:, :128], value[:, :128]
                    ).astype(bf16)
                    spec_s[coil, part, rows, pl.ds(start + 128, 128)] = value[:, 128:].astype(bf16)

    first_row = lax.broadcasted_iota(jnp.int32, (128, half), 0) == 0
    for coil in range(2):
        for nb in range(2):
            cols = pl.ds(nb * half, half)
            from_re = dot(fold_t_ref[...], spec_s[coil, 0, :, cols])
            from_im = dot(fold_t_ref[...], spec_s[coil, 1, :, cols])

            def kept(group):
                rows = slice(group * 128, group * 128 + 128)
                rows_2 = slice(half + group * 128, half + group * 128 + 128)
                re_cos, re_sin = from_re[rows], from_re[rows_2]
                im_cos, im_sin = from_im[rows], from_im[rows_2]
                low = [re_cos + im_sin, im_cos - re_sin]
                high = [re_cos - im_sin, im_cos + re_sin]
                if group == 0:
                    low = [jnp.where(first_row, first, value) for first, value in zip((re_cos, im_cos), low)]
                    high = [jnp.where(first_row, first, value) for first, value in zip((re_sin, im_sin), high)]
                keep_low, keep_high = mask_s[rows, cols], mask_s[rows_2, cols]
                pieces = [low[0] * keep_low, high[0] * keep_high, low[1] * keep_low, high[1] * keep_high]
                return jnp.concatenate([piece.astype(bf16) for piece in pieces], axis=0)

            even = dot(z_even_ref[...], kept(0))
            odd = dot(z_odd_ref[...], kept(1))
            for part in range(2):
                rows = slice(part * half, part * half + half)
                back = ((even[rows] + odd[rows]).astype(bf16), (even[rows] - odd[rows]).astype(bf16))
                at = pl.ds(part * half + nb * 128, 128)
                for block in range(2):
                    even_s[coil, pl.ds(block * half, half), at] = back[block][:, :128]
                    odd_s[coil, pl.ds(block * half, half), at] = back[block][:, 128:]

    for copy in own_copies:
        copy.wait()
    lower = lax.broadcasted_iota(jnp.int32, (half, 128), 1) < 64

    def paired(re, im):
        even = jnp.where(lower, re, pltpu.roll(im, 64, 1))
        odd = jnp.where(lower, pltpu.roll(re, 64, 1), im)
        return even, odd

    for index in range(3):
        even, odd = paired(*(own_s[index, part].reshape(half, 128) for part in range(2)))
        own_ref[index] = jnp.where(core == 0, even, odd).reshape(8, 32, 128)

    for block in range(2):
        rows = pl.ds(block * half, half)
        sums = [[jnp.zeros((half, half), f32) for _ in range(2)] for _ in range(2)]
        for coil in range(2):
            even = dot(even_s[coil, rows, :], y_even_ref[...])
            odd = dot(odd_s[coil, rows, :], y_odd_ref[...])
            for yb in range(2):
                full = even + odd if yb == 0 else even - odd
                re, im = full[:, :half], full[:, half:]
                sens_re, sens_im = (sens(coil, part, block, pl.ds(yb * half, half)) for part in range(2))
                sums[yb][0] += sens_re * re + sens_im * im
                sums[yb][1] += sens_re * im - sens_im * re
        for yb in range(2):
            for lb in range(2):
                lanes = slice(lb * 128, lb * 128 + 128)
                even, odd = paired(sums[yb][0][:, lanes], sums[yb][1][:, lanes])
                slabs = pl.ds(block * 8, 8)
                keep_ref[slabs, yb * 2 + lb] = jnp.where(core == 0, even, odd).reshape(8, 32, 128)
                send_ref[slabs, yb * 2 + lb] = jnp.where(core == 0, odd, even).reshape(8, 32, 128)


def operator(coil, got, mate, fold_tabs, direction, residual, image):
    hbm = pl.BlockSpec(memory_space=pltpu.HBM)
    smem = pl.BlockSpec(memory_space=pltpu.SMEM)
    vmem = pl.BlockSpec(memory_space=pltpu.VMEM)
    return pl.pallas_call(
        operator_kernel,
        in_specs=[smem] + [vmem] * 10 + [hbm] * 3,
        out_specs=[vmem] * 3,
        out_shape=[
            jax.ShapeDtypeStruct((16, 4, 32, 128), jnp.float32),
            jax.ShapeDtypeStruct((16, 4, 32, 128), jnp.float32),
            jax.ShapeDtypeStruct((3, 8, 32, 128), jnp.float32),
        ],
        scratch_shapes=[
            pltpu.VMEM((2, 2, 512, 512), jnp.bfloat16),
            pltpu.VMEM((2, 2, 512, 512), jnp.bfloat16),
            pltpu.VMEM((2, 512, 512), jnp.bfloat16),
            pltpu.VMEM((2, 512, 512), jnp.bfloat16),
            pltpu.VMEM((3, 16, 2, 16, 512), jnp.bfloat16),
            pltpu.VMEM((512, 512), jnp.float32),
            pltpu.VMEM((3, 2, 8, 32, 128), jnp.float32),
            pltpu.SemaphoreType.DMA((3,)),
        ],
        compiler_params=pltpu.CompilerParams(vmem_limit_bytes=32 * 1024 * 1024),
        name="operator",
    )(coil, got, mate, *fold_tabs, direction, residual, image)


def sums_kernel(part_ref, own_ref, applied_ref, sums_ref):
    def body(x, carry):
        rr, da, ra, aa = carry
        total = jnp.zeros(applied_ref.shape[1:], jnp.float32)
        for coil in range(4):
            for pair in range(2):
                total += part_ref[x, pair, coil].astype(jnp.float32)
        direction = own_ref[0, x]
        residual = own_ref[1, x]
        applied = total + ridge_weight * direction
        applied_ref[x] = applied
        return (
            rr + residual * residual,
            da + direction * applied,
            ra + residual * applied,
            aa + applied * applied,
        )

    zero = jnp.zeros(applied_ref.shape[1:], jnp.float32)
    sums = lax.fori_loop(0, applied_ref.shape[0], body, (zero,) * 4)
    lane = lax.broadcasted_iota(jnp.int32, (1, 128), 1)
    row = jnp.zeros((1, 128), jnp.float32)
    for index, value in enumerate(sums):
        row = jnp.where(lane == index, jnp.sum(value), row)
    sums_ref[...] = jnp.broadcast_to(row, sums_ref.shape)


def final_kernel(all_ref, applied_ref, own_ref, img_out, res_out, dir_out):
    total = jnp.sum(all_ref[...], axis=0, keepdims=True)
    rr, da, ra, aa = (total[:, i : i + 1] for i in range(4))
    step = rr / da
    new = rr + step * (step * aa - 2.0 * ra)
    beta = new / rr
    step = step.reshape(1, 1, 1)
    beta = beta.reshape(1, 1, 1)
    direction = own_ref[0]
    img = own_ref[2] + step * direction
    res = own_ref[1] - step * applied_ref[...]
    nxt = res + beta * direction
    for out, value in ((img_out, img), (res_out, res), (dir_out, nxt)):
        out[0] = value[:, :, :64]
        out[1] = value[:, :, 64:]


def on_device(image, residual, direction, sensitivity, sampling):
    fold_tabs = [jnp.asarray(table) for table in fold_tables(512)]
    coil = lax.axis_index("coil").reshape(1)
    mates = [(at, at ^ 1) for at in range(8)]
    same_core = [[at * 16 + to for to in range(16) for at in range(side, 8, 2)] for side in range(2)]
    packed = pack(coil % 2, sensitivity, direction, sampling.T)
    got = lax.all_to_all(packed.reshape(16, 176, 512), "space", 0, 0, tiled=True)
    mate = lax.ppermute(got[:, 128:], "coil", mates)
    keep, send, own = operator(coil, got, mate, fold_tabs, direction, residual, image)
    pair_sum = (keep + lax.ppermute(send, "coil", mates)).astype(jnp.bfloat16)
    parts = lax.all_to_all(
        pair_sum.reshape(64, 32, 128), ("coil", "space"), 0, 0, axis_index_groups=same_core, tiled=True
    )
    whole = pl.BlockSpec(memory_space=pltpu.VMEM)
    params = pltpu.CompilerParams(vmem_limit_bytes=vmem_limit)
    applied, sums = pl.pallas_call(
        sums_kernel,
        in_specs=[whole] * 2,
        out_specs=[whole] * 2,
        out_shape=[
            jax.ShapeDtypeStruct((8, 32, 128), jnp.float32),
            jax.ShapeDtypeStruct((128, 128), jnp.float32),
        ],
        compiler_params=params,
        name="sums",
    )(parts.reshape(8, 2, 4, 32, 128), own)
    everyone = lax.all_to_all(sums, ("space", "coil"), split_axis=0, concat_axis=0, tiled=True)
    outs = pl.pallas_call(
        final_kernel,
        in_specs=[whole] * 3,
        out_specs=[whole] * 3,
        out_shape=[jax.ShapeDtypeStruct((2, 8, 32, 64), jnp.float32)] * 3,
        compiler_params=params,
        name="final",
    )(everyone, applied, own)
    return tuple(outs)


def solution(mesh):
    placed = (
        P(None, None, "space", None),
        P(None, None, "space", None),
        P(None, None, "space", None),
        P(None, "coil", None, "space", None),
        P(None, "space"),
    )
    return jax.shard_map(
        on_device,
        mesh=mesh,
        in_specs=placed,
        out_specs=(P(None, None, "space", "coil"),) * 3,
        check_vma=False,
    )
```

```python
import math

import jax
import jax.numpy as jnp
import ml_dtypes
import numpy as np
from jax import lax
from jax.experimental import pallas as pl
from jax.experimental.pallas import tpu as pltpu
from jax.sharding import PartitionSpec as P

ridge_weight = 0.1
vmem_limit = 8 * 1024 * 1024


def tables(length):
    counter = np.arange(length, dtype=np.int32)
    product_mod = counter[:, None] * counter[None, :] % length
    phase_angle = product_mod.astype(np.float32) * np.float32(2.0 * math.pi / length)
    norm_scale = np.float32(1.0 / math.sqrt(length))
    return np.cos(phase_angle) * norm_scale, np.sin(phase_angle) * norm_scale


def fold_tables(length):
    cos_t, sin_t = tables(length)
    half = length // 2
    even, odd = np.arange(0, half, 2), np.arange(1, half, 2)
    low = np.concatenate([even, odd])
    high = np.where(low == 0, half, length - low)
    sine = sin_t[:, low].copy()
    sine[:, 0] = cos_t[:, half]
    fold = np.concatenate([cos_t[:, low], sine], axis=1)
    order = np.concatenate([low, high])
    pick = np.eye(length, dtype=np.float32)[:, order]
    outs = [fold, fold.T, pick, pick.T]
    for group in (even, odd):
        at = np.concatenate([group, np.where(group == 0, half, length - group)])
        cos_g, sin_g = cos_t[:half, at], sin_t[:half, at]
        block = np.block([[cos_g, -sin_g], [sin_g, cos_g]])
        outs += [block, block.T]
    return [np.ascontiguousarray(out).astype(ml_dtypes.bfloat16) for out in outs]


def pack_kernel(core_ref, sens_ref, dir_ref, mask_ref, out_ref, sens_s, dir_s, mask_s, small_s, in_sems, out_sems):
    core_rows = pl.ds(pl.multiple_of(core_ref[0] * 16, 16), 16)
    small = [
        pltpu.make_async_copy(dir_ref.at[part, :, core_rows, :], dir_s.at[part], in_sems.at[8 + part])
        for part in range(2)
    ]
    small.append(pltpu.make_async_copy(mask_ref.at[core_rows, :], mask_s, in_sems.at[10]))
    pairs = [(part, coil) for part in range(2) for coil in range(4)]
    loads = [
        pltpu.make_async_copy(sens_ref.at[part, coil], sens_s.at[part, coil], in_sems.at[part * 4 + coil])
        for part, coil in pairs
    ]
    stores = [
        pltpu.make_async_copy(
            sens_s.at[part, coil],
            out_ref.at[:, coil // 2, pl.ds((part * 2 + coil % 2) * 32, 32), :],
            out_sems.at[part * 4 + coil],
        )
        for part, coil in pairs
    ]
    stores += [
        pltpu.make_async_copy(small_s, out_ref.at[:, half, pl.ds(128, 48), :], out_sems.at[8 + half])
        for half in range(2)
    ]
    for copy in small + loads:
        copy.start()
    for copy in small:
        copy.wait()
    kept = mask_s[...].astype(jnp.bfloat16)
    for x in range(8):
        for part in range(2):
            small_s[x, pl.ds(part * 16, 16), :] = dir_s[part, x].astype(jnp.bfloat16)
        small_s[x, pl.ds(32, 16), :] = kept
    for copy in stores[8:]:
        copy.start()
    for load, store in zip(loads, stores):
        load.wait()
        store.start()
    for copy in stores:
        copy.wait()


def pack(core, sensitivity, direction, mask_t):
    hbm = pl.BlockSpec(memory_space=pltpu.HBM)
    return pl.pallas_call(
        pack_kernel,
        in_specs=[pl.BlockSpec(memory_space=pltpu.SMEM), hbm, hbm, hbm],
        out_specs=hbm,
        out_shape=jax.ShapeDtypeStruct((8, 2, 176, 512), jnp.bfloat16),
        scratch_shapes=[
            pltpu.VMEM((2, 4, 8, 32, 512), jnp.bfloat16),
            pltpu.VMEM((2, 8, 16, 512), jnp.float32),
            pltpu.VMEM((16, 512), jnp.int32),
            pltpu.VMEM((8, 48, 512), jnp.bfloat16),
            pltpu.SemaphoreType.DMA((11,)),
            pltpu.SemaphoreType.DMA((10,)),
        ],
        compiler_params=pltpu.CompilerParams(vmem_limit_bytes=60 * 1024 * 1024),
        name="pack",
    )(core, sensitivity, direction, mask_t)


def dot(left, right):
    return jnp.dot(left, right, preferred_element_type=jnp.float32)


def spectrum_rows(got_ref, dir_parts, core, fold_ref, image_s, store):
    half = 256
    first_lane = lax.broadcasted_iota(jnp.int32, (half, 128), 1) == 0
    for coil in range(2):
        for yb in range(2):
            cols = pl.ds(yb * half, half)
            dir_re, dir_im = (part[:, :, cols].reshape(half, half).astype(jnp.float32) for part in dir_parts)
            sens_re, sens_im = (
                got_ref[:, pl.ds(pl.multiple_of((part * 2 + coil) * 32 + core * 16, 16), 16), cols]
                .reshape(half, half)
                .astype(jnp.float32)
                for part in range(2)
            )
            image_s[coil, 0, :, cols] = (sens_re * dir_re - sens_im * dir_im).astype(jnp.bfloat16)
            image_s[coil, 1, :, cols] = (sens_re * dir_im + sens_im * dir_re).astype(jnp.bfloat16)
        from_re = dot(image_s[coil, 0], fold_ref[...])
        from_im = dot(image_s[coil, 1], fold_ref[...])
        re_cos, re_sin = from_re[:, :half], from_re[:, half:]
        im_cos, im_sin = from_im[:, :half], from_im[:, half:]
        low = (re_cos + im_sin, im_cos - re_sin)
        high = (re_cos - im_sin, im_cos + re_sin)
        low_first = (re_cos, im_cos)
        high_first = (re_sin, im_sin)
        for part in range(2):
            for start, value, first in ((0, low[part], low_first[part]), (half, high[part], high_first[part])):
                edge = jnp.where(first_lane, first[:, :128], value[:, :128])
                store(coil, part, start, edge.astype(jnp.bfloat16))
                store(coil, part, start + 128, value[:, 128:].astype(jnp.bfloat16))


def own_rows_kernel(coil_ref, got_ref, fold_ref, out_ref, image_s):
    def store(coil, part, start, value):
        out_ref[coil, part, :, :, pl.ds(start, 128)] = value.reshape(16, 16, 128)

    dir_parts = [got_ref.at[:, pl.ds(128 + part * 16, 16), :] for part in range(2)]
    spectrum_rows(got_ref, dir_parts, coil_ref[0] % 2, fold_ref, image_s, store)


def own_rows(coil, got, fold):
    vmem = pl.BlockSpec(memory_space=pltpu.VMEM)
    return pl.pallas_call(
        own_rows_kernel,
        in_specs=[pl.BlockSpec(memory_space=pltpu.SMEM), vmem, vmem],
        out_specs=vmem,
        out_shape=jax.ShapeDtypeStruct((2, 2, 16, 16, 512), jnp.bfloat16),
        scratch_shapes=[pltpu.VMEM((2, 2, 256, 512), jnp.bfloat16)],
        compiler_params=pltpu.CompilerParams(vmem_limit_bytes=16 * 1024 * 1024),
        name="own_rows",
    )(coil, got, fold)


def operator_kernel(
    coil_ref, got_ref, mate_ref, ready_ref, fold_ref, fold_t_ref, pick_ref, pick_t_ref,
    z_even_ref, y_even_ref, z_odd_ref, y_odd_ref, dir_ref, res_ref, img_ref,
    keep_ref, send_ref, own_ref,
    image_s, spec_s, even_s, odd_s, mask_t_s, mask_s, own_s, sems,
):
    size = 512
    half = 256
    f32 = jnp.float32
    bf16 = jnp.bfloat16
    core = coil_ref[0] % 2
    own_lanes = pl.ds(pl.multiple_of(coil_ref[0] // 2 * 128, 128), 128)
    own_copies = [
        pltpu.make_async_copy(ref.at[:, :, :, own_lanes], own_s.at[index], sems.at[index])
        for index, ref in enumerate((dir_ref, res_ref, img_ref))
    ]
    for copy in own_copies:
        copy.start()

    mask_t_s[:, core] = got_ref[:, pl.ds(160, 16), :]
    mask_t_s[:, 1 - core] = mate_ref[:, pl.ds(32, 16), :]
    mask_t = dot(pick_t_ref[...], mask_t_s[...].reshape(size, size)).astype(bf16)
    mask_s[...] = dot(mask_t, pick_ref[...]).T

    def store(coil, part, start, value):
        spec_s[coil, part, :, 1 - core, :, pl.ds(start, 128)] = value.reshape(16, 16, 128)

    dir_parts = [mate_ref.at[:, pl.ds(part * 16, 16), :] for part in range(2)]
    spectrum_rows(got_ref, dir_parts, 1 - core, fold_ref, image_s, store)
    for coil in range(2):
        for part in range(2):
            spec_s[coil, part, :, core] = ready_ref[coil, part]

    def sens(coil, part, block, lanes):
        rows = got_ref[pl.ds(block * 8, 8), pl.ds((part * 2 + coil) * 32, 32), lanes]
        return rows.reshape(half, -1).astype(f32)

    first_row = lax.broadcasted_iota(jnp.int32, (128, half), 0) == 0
    for coil in range(2):
        for nb in range(2):
            cols = pl.ds(nb * half, half)
            from_re = dot(fold_t_ref[...], spec_s[coil, 0, :, :, :, cols].reshape(size, half))
            from_im = dot(fold_t_ref[...], spec_s[coil, 1, :, :, :, cols].reshape(size, half))

            def kept(group):
                rows = slice(group * 128, group * 128 + 128)
                rows_2 = slice(half + group * 128, half + group * 128 + 128)
                re_cos, re_sin = from_re[rows], from_re[rows_2]
                im_cos, im_sin = from_im[rows], from_im[rows_2]
                low = [re_cos + im_sin, im_cos - re_sin]
                high = [re_cos - im_sin, im_cos + re_sin]
                if group == 0:
                    low = [jnp.where(first_row, first, value) for first, value in zip((re_cos, im_cos), low)]
                    high = [jnp.where(first_row, first, value) for first, value in zip((re_sin, im_sin), high)]
                keep_low, keep_high = mask_s[rows, cols], mask_s[rows_2, cols]
                pieces = [low[0] * keep_low, high[0] * keep_high, low[1] * keep_low, high[1] * keep_high]
                return jnp.concatenate([piece.astype(bf16) for piece in pieces], axis=0)

            even = dot(z_even_ref[...], kept(0))
            odd = dot(z_odd_ref[...], kept(1))
            for part in range(2):
                rows = slice(part * half, part * half + half)
                back = ((even[rows] + odd[rows]).astype(bf16), (even[rows] - odd[rows]).astype(bf16))
                at = pl.ds(part * half + nb * 128, 128)
                for block in range(2):
                    even_s[coil, pl.ds(block * half, half), at] = back[block][:, :128]
                    odd_s[coil, pl.ds(block * half, half), at] = back[block][:, 128:]

    for copy in own_copies:
        copy.wait()
    lower = lax.broadcasted_iota(jnp.int32, (half, 128), 1) < 64

    def paired(re, im):
        even = jnp.where(lower, re, pltpu.roll(im, 64, 1))
        odd = jnp.where(lower, pltpu.roll(re, 64, 1), im)
        return even, odd

    for index in range(3):
        even, odd = paired(*(own_s[index, part].reshape(half, 128) for part in range(2)))
        own_ref[index] = jnp.where(core == 0, even, odd).reshape(8, 32, 128)

    for block in range(2):
        rows = pl.ds(block * half, half)
        sums = [[jnp.zeros((half, half), f32) for _ in range(2)] for _ in range(2)]
        for coil in range(2):
            even = dot(even_s[coil, rows, :], y_even_ref[...])
            odd = dot(odd_s[coil, rows, :], y_odd_ref[...])
            for yb in range(2):
                full = even + odd if yb == 0 else even - odd
                re, im = full[:, :half], full[:, half:]
                sens_re, sens_im = (sens(coil, part, block, pl.ds(yb * half, half)) for part in range(2))
                sums[yb][0] += sens_re * re + sens_im * im
                sums[yb][1] += sens_re * im - sens_im * re
        for yb in range(2):
            for lb in range(2):
                lanes = slice(lb * 128, lb * 128 + 128)
                even, odd = paired(sums[yb][0][:, lanes], sums[yb][1][:, lanes])
                slabs = pl.ds(block * 8, 8)
                keep_ref[slabs, yb * 2 + lb] = jnp.where(core == 0, even, odd).reshape(8, 32, 128)
                send_ref[slabs, yb * 2 + lb] = jnp.where(core == 0, odd, even).reshape(8, 32, 128)


def operator(coil, got, mate, ready, fold_tabs, direction, residual, image):
    hbm = pl.BlockSpec(memory_space=pltpu.HBM)
    smem = pl.BlockSpec(memory_space=pltpu.SMEM)
    vmem = pl.BlockSpec(memory_space=pltpu.VMEM)
    return pl.pallas_call(
        operator_kernel,
        in_specs=[smem] + [vmem] * 11 + [hbm] * 3,
        out_specs=[vmem] * 3,
        out_shape=[
            jax.ShapeDtypeStruct((16, 4, 32, 128), jnp.float32),
            jax.ShapeDtypeStruct((16, 4, 32, 128), jnp.float32),
            jax.ShapeDtypeStruct((3, 8, 32, 128), jnp.float32),
        ],
        scratch_shapes=[
            pltpu.VMEM((2, 2, 256, 512), jnp.bfloat16),
            pltpu.VMEM((2, 2, 16, 2, 16, 512), jnp.bfloat16),
            pltpu.VMEM((2, 512, 512), jnp.bfloat16),
            pltpu.VMEM((2, 512, 512), jnp.bfloat16),
            pltpu.VMEM((16, 2, 16, 512), jnp.bfloat16),
            pltpu.VMEM((512, 512), jnp.float32),
            pltpu.VMEM((3, 2, 8, 32, 128), jnp.float32),
            pltpu.SemaphoreType.DMA((3,)),
        ],
        compiler_params=pltpu.CompilerParams(vmem_limit_bytes=32 * 1024 * 1024),
        name="operator",
    )(coil, got, mate, ready, *fold_tabs, direction, residual, image)


def sums_kernel(part_ref, own_ref, applied_ref, sums_ref):
    def body(x, carry):
        rr, da, ra, aa = carry
        total = jnp.zeros(applied_ref.shape[1:], jnp.float32)
        for coil in range(4):
            for pair in range(2):
                total += part_ref[x, pair, coil].astype(jnp.float32)
        direction = own_ref[0, x]
        residual = own_ref[1, x]
        applied = total + ridge_weight * direction
        applied_ref[x] = applied
        return (
            rr + residual * residual,
            da + direction * applied,
            ra + residual * applied,
            aa + applied * applied,
        )

    zero = jnp.zeros(applied_ref.shape[1:], jnp.float32)
    sums = lax.fori_loop(0, applied_ref.shape[0], body, (zero,) * 4)
    lane = lax.broadcasted_iota(jnp.int32, (1, 128), 1)
    row = jnp.zeros((1, 128), jnp.float32)
    for index, value in enumerate(sums):
        row = jnp.where(lane == index, jnp.sum(value), row)
    sums_ref[...] = jnp.broadcast_to(row, sums_ref.shape)


def final_kernel(all_ref, applied_ref, own_ref, img_out, res_out, dir_out):
    total = jnp.sum(all_ref[...], axis=0, keepdims=True)
    rr, da, ra, aa = (total[:, i : i + 1] for i in range(4))
    step = rr / da
    new = rr + step * (step * aa - 2.0 * ra)
    beta = new / rr
    step = step.reshape(1, 1, 1)
    beta = beta.reshape(1, 1, 1)
    direction = own_ref[0]
    img = own_ref[2] + step * direction
    res = own_ref[1] - step * applied_ref[...]
    nxt = res + beta * direction
    for out, value in ((img_out, img), (res_out, res), (dir_out, nxt)):
        out[0] = value[:, :, :64]
        out[1] = value[:, :, 64:]


def on_device(image, residual, direction, sensitivity, sampling):
    fold_tabs = [jnp.asarray(table) for table in fold_tables(512)]
    coil = lax.axis_index("coil").reshape(1)
    mates = [(at, at ^ 1) for at in range(8)]
    same_core = [[at * 16 + to for to in range(16) for at in range(side, 8, 2)] for side in range(2)]
    packed = pack(coil % 2, sensitivity, direction, sampling.T)
    got = lax.all_to_all(packed.reshape(16, 176, 512), "space", 0, 0, tiled=True)
    mate = lax.ppermute(got[:, 128:], "coil", mates)
    ready = own_rows(coil, got, fold_tabs[0])
    keep, send, own = operator(coil, got, mate, ready, fold_tabs, direction, residual, image)
    pair_sum = (keep + lax.ppermute(send, "coil", mates)).astype(jnp.bfloat16)
    parts = lax.all_to_all(
        pair_sum.reshape(64, 32, 128), ("coil", "space"), 0, 0, axis_index_groups=same_core, tiled=True
    )
    whole = pl.BlockSpec(memory_space=pltpu.VMEM)
    params = pltpu.CompilerParams(vmem_limit_bytes=vmem_limit)
    applied, sums = pl.pallas_call(
        sums_kernel,
        in_specs=[whole] * 2,
        out_specs=[whole] * 2,
        out_shape=[
            jax.ShapeDtypeStruct((8, 32, 128), jnp.float32),
            jax.ShapeDtypeStruct((128, 128), jnp.float32),
        ],
        compiler_params=params,
        name="sums",
    )(parts.reshape(8, 2, 4, 32, 128), own)
    everyone = lax.all_to_all(sums, ("space", "coil"), split_axis=0, concat_axis=0, tiled=True)
    outs = pl.pallas_call(
        final_kernel,
        in_specs=[whole] * 3,
        out_specs=[whole] * 3,
        out_shape=[jax.ShapeDtypeStruct((2, 8, 32, 64), jnp.float32)] * 3,
        compiler_params=params,
        name="final",
    )(everyone, applied, own)
    return tuple(outs)


def solution(mesh):
    placed = (
        P(None, None, "space", None),
        P(None, None, "space", None),
        P(None, None, "space", None),
        P(None, "coil", None, "space", None),
        P(None, "space"),
    )
    return jax.shard_map(
        on_device,
        mesh=mesh,
        in_specs=placed,
        out_specs=(P(None, None, "space", "coil"),) * 3,
        check_vma=False,
    )
```

```python
import math

import jax
import jax.numpy as jnp
import ml_dtypes
import numpy as np
from jax import lax
from jax.experimental import pallas as pl
from jax.experimental.pallas import tpu as pltpu
from jax.sharding import PartitionSpec as P

ridge_weight = 0.1
vmem_limit = 8 * 1024 * 1024


def tables(length):
    counter = np.arange(length, dtype=np.int32)
    product_mod = counter[:, None] * counter[None, :] % length
    phase_angle = product_mod.astype(np.float32) * np.float32(2.0 * math.pi / length)
    norm_scale = np.float32(1.0 / math.sqrt(length))
    return np.cos(phase_angle) * norm_scale, np.sin(phase_angle) * norm_scale


def fold_tables(length):
    cos_t, sin_t = tables(length)
    half = length // 2
    even, odd = np.arange(0, half, 2), np.arange(1, half, 2)
    low = np.concatenate([even, odd])
    high = np.where(low == 0, half, length - low)
    sine = sin_t[:, low].copy()
    sine[:, 0] = cos_t[:, half]
    fold = np.concatenate([cos_t[:, low], sine], axis=1)
    order = np.concatenate([low, high])
    pick = np.eye(length, dtype=np.float32)[:, order]
    outs = [fold, fold.T, pick, pick.T]
    for group in (even, odd):
        at = np.concatenate([group, np.where(group == 0, half, length - group)])
        cos_g, sin_g = cos_t[:half, at], sin_t[:half, at]
        block = np.block([[cos_g, -sin_g], [sin_g, cos_g]])
        outs += [block, block.T]
    return [np.ascontiguousarray(out).astype(ml_dtypes.bfloat16) for out in outs]


def pack_kernel(core_ref, sens_ref, dir_ref, mask_ref, out_ref, sens_s, dir_s, mask_s, small_s, in_sems, out_sems):
    core_rows = pl.ds(pl.multiple_of(core_ref[0] * 16, 16), 16)
    small = [
        pltpu.make_async_copy(dir_ref.at[part, :, core_rows, :], dir_s.at[part], in_sems.at[8 + part])
        for part in range(2)
    ]
    small.append(pltpu.make_async_copy(mask_ref.at[core_rows, :], mask_s, in_sems.at[10]))
    pairs = [(part, coil) for part in range(2) for coil in range(4)]
    loads = [
        pltpu.make_async_copy(sens_ref.at[part, coil], sens_s.at[part, coil], in_sems.at[part * 4 + coil])
        for part, coil in pairs
    ]
    stores = [
        pltpu.make_async_copy(
            sens_s.at[part, coil],
            out_ref.at[:, coil // 2, pl.ds((part * 2 + coil % 2) * 32, 32), :],
            out_sems.at[part * 4 + coil],
        )
        for part, coil in pairs
    ]
    stores += [
        pltpu.make_async_copy(small_s, out_ref.at[:, half, pl.ds(128, 48), :], out_sems.at[8 + half])
        for half in range(2)
    ]
    for copy in small + loads:
        copy.start()
    for copy in small:
        copy.wait()
    kept = mask_s[...].astype(jnp.bfloat16)
    for x in range(8):
        for part in range(2):
            small_s[x, pl.ds(part * 16, 16), :] = dir_s[part, x].astype(jnp.bfloat16)
        small_s[x, pl.ds(32, 16), :] = kept
    for copy in stores[8:]:
        copy.start()
    for load, store in zip(loads, stores):
        load.wait()
        store.start()
    for copy in stores:
        copy.wait()


def pack(core, sensitivity, direction, mask_t):
    hbm = pl.BlockSpec(memory_space=pltpu.HBM)
    return pl.pallas_call(
        pack_kernel,
        in_specs=[pl.BlockSpec(memory_space=pltpu.SMEM), hbm, hbm, hbm],
        out_specs=hbm,
        out_shape=jax.ShapeDtypeStruct((8, 2, 176, 512), jnp.bfloat16),
        scratch_shapes=[
            pltpu.VMEM((2, 4, 8, 32, 512), jnp.bfloat16),
            pltpu.VMEM((2, 8, 16, 512), jnp.float32),
            pltpu.VMEM((16, 512), jnp.int32),
            pltpu.VMEM((8, 48, 512), jnp.bfloat16),
            pltpu.SemaphoreType.DMA((11,)),
            pltpu.SemaphoreType.DMA((10,)),
        ],
        compiler_params=pltpu.CompilerParams(vmem_limit_bytes=60 * 1024 * 1024),
        name="pack",
    )(core, sensitivity, direction, mask_t)


def dot(left, right):
    return jnp.dot(left, right, preferred_element_type=jnp.float32)


def spectrum_rows(got_ref, dir_parts, core, fold_ref, image_s, store):
    half = 256
    first_lane = lax.broadcasted_iota(jnp.int32, (half, 128), 1) == 0
    for coil in range(2):
        for yb in range(2):
            cols = pl.ds(yb * half, half)
            dir_re, dir_im = (part[:, :, cols].reshape(half, half).astype(jnp.float32) for part in dir_parts)
            sens_re, sens_im = (
                got_ref[:, pl.ds(pl.multiple_of((part * 2 + coil) * 32 + core * 16, 16), 16), cols]
                .reshape(half, half)
                .astype(jnp.float32)
                for part in range(2)
            )
            image_s[coil, 0, :, cols] = (sens_re * dir_re - sens_im * dir_im).astype(jnp.bfloat16)
            image_s[coil, 1, :, cols] = (sens_re * dir_im + sens_im * dir_re).astype(jnp.bfloat16)
    for coil in range(2):
        from_re = dot(image_s[coil, 0], fold_ref[...])
        from_im = dot(image_s[coil, 1], fold_ref[...])
        re_cos, re_sin = from_re[:, :half], from_re[:, half:]
        im_cos, im_sin = from_im[:, :half], from_im[:, half:]
        low = (re_cos + im_sin, im_cos - re_sin)
        high = (re_cos - im_sin, im_cos + re_sin)
        low_first = (re_cos, im_cos)
        high_first = (re_sin, im_sin)
        for part in range(2):
            for start, value, first in ((0, low[part], low_first[part]), (half, high[part], high_first[part])):
                edge = jnp.where(first_lane, first[:, :128], value[:, :128])
                store(coil, part, start, edge.astype(jnp.bfloat16))
                store(coil, part, start + 128, value[:, 128:].astype(jnp.bfloat16))


def own_rows_kernel(
    coil_ref, got_ref, fold_ref, pick_ref, dir_ref, res_ref, img_ref, out_ref, mask_ref, own_ref, image_s, own_s, sems
):
    core = coil_ref[0] % 2
    own_lanes = pl.ds(pl.multiple_of(coil_ref[0] // 2 * 128, 128), 128)
    own_copies = [
        pltpu.make_async_copy(ref.at[:, :, :, own_lanes], own_s.at[index], sems.at[index])
        for index, ref in enumerate((dir_ref, res_ref, img_ref))
    ]
    for copy in own_copies:
        copy.start()

    def store(coil, part, start, value):
        out_ref[coil, part, :, :, pl.ds(start, 128)] = value.reshape(16, 16, 128)

    dir_parts = [got_ref.at[:, pl.ds(128 + part * 16, 16), :] for part in range(2)]
    spectrum_rows(got_ref, dir_parts, core, fold_ref, image_s, store)
    mask_ref[...] = mask_columns(got_ref[:, pl.ds(160, 16), :], pick_ref)
    for copy in own_copies:
        copy.wait()
    for index in range(3):
        even, odd = paired(*(own_s[index, part].reshape(256, 128) for part in range(2)))
        own_ref[index] = jnp.where(core == 0, even, odd).reshape(8, 32, 128)


def mask_columns(rows, pick_ref):
    return dot(rows.reshape(256, 512), pick_ref[...]).astype(jnp.bfloat16).reshape(16, 16, 512)


def paired(re, im):
    lower = lax.broadcasted_iota(jnp.int32, re.shape, 1) < 64
    moved = pltpu.roll(jnp.where(lower, im, re), 64, 1)
    return jnp.where(lower, re, moved), jnp.where(lower, moved, im)


def own_rows(coil, got, fold, pick, direction, residual, image):
    hbm = pl.BlockSpec(memory_space=pltpu.HBM)
    vmem = pl.BlockSpec(memory_space=pltpu.VMEM)
    return pl.pallas_call(
        own_rows_kernel,
        in_specs=[pl.BlockSpec(memory_space=pltpu.SMEM)] + [vmem] * 3 + [hbm] * 3,
        out_specs=[vmem] * 3,
        out_shape=[
            jax.ShapeDtypeStruct((2, 2, 16, 16, 512), jnp.bfloat16),
            jax.ShapeDtypeStruct((16, 16, 512), jnp.bfloat16),
            jax.ShapeDtypeStruct((3, 8, 32, 128), jnp.float32),
        ],
        scratch_shapes=[
            pltpu.VMEM((2, 2, 256, 512), jnp.bfloat16),
            pltpu.VMEM((3, 2, 8, 32, 128), jnp.float32),
            pltpu.SemaphoreType.DMA((3,)),
        ],
        compiler_params=pltpu.CompilerParams(vmem_limit_bytes=16 * 1024 * 1024),
        name="own_rows",
    )(coil, got, fold, pick, direction, residual, image)


def operator_kernel(
    coil_ref, got_ref, mate_ref, ready_ref, mask_ref, fold_ref, fold_t_ref, pick_ref, pick_t_ref,
    z_even_ref, y_even_ref, z_odd_ref, y_odd_ref,
    keep_ref, send_ref,
    image_s, spec_s, even_s, odd_s, mask_t_s, mask_s,
):
    size = 512
    half = 256
    f32 = jnp.float32
    bf16 = jnp.bfloat16
    core = coil_ref[0] % 2
    def store(coil, part, start, value):
        spec_s[coil, part, :, 1 - core, :, pl.ds(start, 128)] = value.reshape(16, 16, 128)

    dir_parts = [mate_ref.at[:, pl.ds(part * 16, 16), :] for part in range(2)]
    spectrum_rows(got_ref, dir_parts, 1 - core, fold_ref, image_s, store)
    for coil in range(2):
        for part in range(2):
            spec_s[coil, part, :, core] = ready_ref[coil, part]

    mask_t_s[:, core] = mask_ref[...]
    mask_t_s[:, 1 - core] = mask_columns(mate_ref[:, pl.ds(32, 16), :], pick_ref)
    mask_s[...] = dot(pick_t_ref[...], mask_t_s[...].reshape(size, size)).T

    def sens(coil, part, block, lanes):
        rows = got_ref[pl.ds(block * 8, 8), pl.ds((part * 2 + coil) * 32, 32), lanes]
        return rows.reshape(half, -1).astype(f32)

    first_row = lax.broadcasted_iota(jnp.int32, (128, half), 0) == 0
    for coil in range(2):
        full_re = dot(fold_t_ref[...], spec_s[coil, 0].reshape(size, size))
        full_im = dot(fold_t_ref[...], spec_s[coil, 1].reshape(size, size))
        for nb in range(2):
            cols = pl.ds(nb * half, half)
            from_re = full_re[:, nb * half : nb * half + half]
            from_im = full_im[:, nb * half : nb * half + half]

            def kept(group):
                rows = slice(group * 128, group * 128 + 128)
                rows_2 = slice(half + group * 128, half + group * 128 + 128)
                re_cos, re_sin = from_re[rows], from_re[rows_2]
                im_cos, im_sin = from_im[rows], from_im[rows_2]
                low = [re_cos + im_sin, im_cos - re_sin]
                high = [re_cos - im_sin, im_cos + re_sin]
                if group == 0:
                    low = [jnp.where(first_row, first, value) for first, value in zip((re_cos, im_cos), low)]
                    high = [jnp.where(first_row, first, value) for first, value in zip((re_sin, im_sin), high)]
                keep_low, keep_high = mask_s[rows, cols], mask_s[rows_2, cols]
                pieces = [low[0] * keep_low, high[0] * keep_high, low[1] * keep_low, high[1] * keep_high]
                return jnp.concatenate([piece.astype(bf16) for piece in pieces], axis=0)

            even = dot(z_even_ref[...], kept(0))
            odd = dot(z_odd_ref[...], kept(1))
            for part in range(2):
                rows = slice(part * half, part * half + half)
                back = ((even[rows] + odd[rows]).astype(bf16), (even[rows] - odd[rows]).astype(bf16))
                at = pl.ds(part * half + nb * 128, 128)
                for block in range(2):
                    even_s[coil, pl.ds(block * half, half), at] = back[block][:, :128]
                    odd_s[coil, pl.ds(block * half, half), at] = back[block][:, 128:]

    for block in range(2):
        rows = pl.ds(block * half, half)
        sums = [[jnp.zeros((half, half), f32) for _ in range(2)] for _ in range(2)]
        for coil in range(2):
            even = dot(even_s[coil, rows, :], y_even_ref[...])
            odd = dot(odd_s[coil, rows, :], y_odd_ref[...])
            for yb in range(2):
                full = even + odd if yb == 0 else even - odd
                re, im = full[:, :half], full[:, half:]
                sens_re, sens_im = (sens(coil, part, block, pl.ds(yb * half, half)) for part in range(2))
                sums[yb][0] += sens_re * re + sens_im * im
                sums[yb][1] += sens_re * im - sens_im * re
        for yb in range(2):
            for lb in range(2):
                lanes = slice(lb * 128, lb * 128 + 128)
                even, odd = paired(sums[yb][0][:, lanes], sums[yb][1][:, lanes])
                slabs = pl.ds(block * 8, 8)
                keep_ref[slabs, yb * 2 + lb] = jnp.where(core == 0, even, odd).reshape(8, 32, 128)
                send_ref[slabs, yb * 2 + lb] = jnp.where(core == 0, odd, even).reshape(8, 32, 128).astype(bf16)


def operator(coil, got, mate, ready, mask, fold_tabs):
    smem = pl.BlockSpec(memory_space=pltpu.SMEM)
    vmem = pl.BlockSpec(memory_space=pltpu.VMEM)
    return pl.pallas_call(
        operator_kernel,
        in_specs=[smem] + [vmem] * 12,
        out_specs=[vmem] * 2,
        out_shape=[
            jax.ShapeDtypeStruct((16, 4, 32, 128), jnp.float32),
            jax.ShapeDtypeStruct((16, 4, 32, 128), jnp.bfloat16),
        ],
        scratch_shapes=[
            pltpu.VMEM((2, 2, 256, 512), jnp.bfloat16),
            pltpu.VMEM((2, 2, 16, 2, 16, 512), jnp.bfloat16),
            pltpu.VMEM((2, 512, 512), jnp.bfloat16),
            pltpu.VMEM((2, 512, 512), jnp.bfloat16),
            pltpu.VMEM((16, 2, 16, 512), jnp.bfloat16),
            pltpu.VMEM((512, 512), jnp.float32),
        ],
        compiler_params=pltpu.CompilerParams(vmem_limit_bytes=32 * 1024 * 1024),
        name="operator",
    )(coil, got, mate, ready, mask, *fold_tabs)


def sums_kernel(part_ref, own_ref, applied_ref, sums_ref):
    def body(x, carry):
        rr, da, ra, aa = carry
        total = jnp.zeros(applied_ref.shape[1:], jnp.float32)
        for coil in range(4):
            for pair in range(2):
                total += part_ref[x, pair, coil].astype(jnp.float32)
        direction = own_ref[0, x]
        residual = own_ref[1, x]
        applied = total + ridge_weight * direction
        applied_ref[x] = applied
        return (
            rr + residual * residual,
            da + direction * applied,
            ra + residual * applied,
            aa + applied * applied,
        )

    zero = jnp.zeros(applied_ref.shape[1:], jnp.float32)
    sums = lax.fori_loop(0, applied_ref.shape[0], body, (zero,) * 4)
    lane = lax.broadcasted_iota(jnp.int32, (1, 128), 1)
    row = jnp.zeros((1, 128), jnp.float32)
    for index, value in enumerate(sums):
        row = jnp.where(lane == index, jnp.sum(value), row)
    sums_ref[...] = jnp.broadcast_to(row, sums_ref.shape)


def final_kernel(all_ref, applied_ref, own_ref, img_out, res_out, dir_out):
    total = jnp.sum(all_ref[...], axis=0, keepdims=True)
    rr, da, ra, aa = (total[:, i : i + 1] for i in range(4))
    step = rr / da
    new = rr + step * (step * aa - 2.0 * ra)
    beta = new / rr
    step = step.reshape(1, 1, 1)
    beta = beta.reshape(1, 1, 1)
    direction = own_ref[0]
    img = own_ref[2] + step * direction
    res = own_ref[1] - step * applied_ref[...]
    nxt = res + beta * direction
    for out, value in ((img_out, img), (res_out, res), (dir_out, nxt)):
        out[0] = value[:, :, :64]
        out[1] = value[:, :, 64:]


def on_device(image, residual, direction, sensitivity, sampling):
    fold_tabs = [jnp.asarray(table) for table in fold_tables(512)]
    coil = lax.axis_index("coil").reshape(1)
    mates = [(at, at ^ 1) for at in range(8)]
    same_core = [[at * 16 + to for to in range(16) for at in range(side, 8, 2)] for side in range(2)]
    packed = pack(coil % 2, sensitivity, direction, sampling.T)
    got = lax.all_to_all(packed.reshape(16, 176, 512), "space", 0, 0, tiled=True)
    mate = lax.ppermute(got[:, 128:], "coil", mates)
    ready, mask, own = own_rows(coil, got, fold_tabs[0], fold_tabs[2], direction, residual, image)
    keep, send = operator(coil, got, mate, ready, mask, fold_tabs)
    pair_sum = (keep + lax.ppermute(send, "coil", mates)).astype(jnp.bfloat16)
    parts = lax.all_to_all(
        pair_sum.reshape(64, 32, 128), ("coil", "space"), 0, 0, axis_index_groups=same_core, tiled=True
    )
    whole = pl.BlockSpec(memory_space=pltpu.VMEM)
    params = pltpu.CompilerParams(vmem_limit_bytes=vmem_limit)
    applied, sums = pl.pallas_call(
        sums_kernel,
        in_specs=[whole] * 2,
        out_specs=[whole] * 2,
        out_shape=[
            jax.ShapeDtypeStruct((8, 32, 128), jnp.float32),
            jax.ShapeDtypeStruct((128, 128), jnp.float32),
        ],
        compiler_params=params,
        name="sums",
    )(parts.reshape(8, 2, 4, 32, 128), own)
    everyone = lax.all_to_all(sums, ("space", "coil"), split_axis=0, concat_axis=0, tiled=True)
    outs = pl.pallas_call(
        final_kernel,
        in_specs=[whole] * 3,
        out_specs=[whole] * 3,
        out_shape=[jax.ShapeDtypeStruct((2, 8, 32, 64), jnp.float32)] * 3,
        compiler_params=params,
        name="final",
    )(everyone, applied, own)
    return tuple(outs)


def solution(mesh):
    placed = (
        P(None, None, "space", None),
        P(None, None, "space", None),
        P(None, None, "space", None),
        P(None, "coil", None, "space", None),
        P(None, "space"),
    )
    return jax.shard_map(
        on_device,
        mesh=mesh,
        in_specs=placed,
        out_specs=(P(None, None, "space", "coil"),) * 3,
        check_vma=False,
    )
```

```python
import math

import jax
import jax.numpy as jnp
import ml_dtypes
import numpy as np
from jax import lax
from jax.experimental import pallas as pl
from jax.experimental.pallas import tpu as pltpu
from jax.sharding import PartitionSpec as P

ridge_weight = 0.1
vmem_limit = 8 * 1024 * 1024


def tables(length):
    counter = np.arange(length, dtype=np.int32)
    product_mod = counter[:, None] * counter[None, :] % length
    phase_angle = product_mod.astype(np.float32) * np.float32(2.0 * math.pi / length)
    norm_scale = np.float32(1.0 / math.sqrt(length))
    return np.cos(phase_angle) * norm_scale, np.sin(phase_angle) * norm_scale


QUARTERS = ((0, 0), (2, 3), (1, 1), (3, 2))


def fold_tables(length):
    cos_t, sin_t = tables(length)
    half = length // 2
    low = np.concatenate([np.arange(rest, half, 4) for rest in (0, 2, 1, 3)])
    high = np.where(low == 0, half, length - low)
    sine = sin_t[:, low].copy()
    sine[:, 0] = cos_t[:, half]
    fold = np.concatenate([cos_t[:, low], sine], axis=1)
    pick = np.eye(length, dtype=np.float32)[:, np.concatenate([low, high])]

    def inverse(rows, at):
        cos_g, sin_g = cos_t[:rows, at], sin_t[:rows, at]
        return np.block([[cos_g, -sin_g], [sin_g, cos_g]])

    quarter = half // 4
    outs = [fold, fold.T, pick, pick.T]
    outs.append(
        np.stack(
            [
                inverse(half // 2, np.concatenate([low[a * quarter :][:quarter], high[b * quarter :][:quarter]]))
                for a, b in QUARTERS
            ]
        )
    )
    for start in (0, half // 2):
        group = slice(start, start + half // 2)
        outs.append(inverse(half, np.concatenate([low[group], high[group]])).T)
    return [np.ascontiguousarray(out).astype(ml_dtypes.bfloat16) for out in outs]


def pack_kernel(core_ref, sens_ref, dir_ref, mask_ref, out_ref, sens_s, dir_s, mask_s, small_s, in_sems, out_sems):
    core_rows = pl.ds(pl.multiple_of(core_ref[0] * 16, 16), 16)
    small = [
        pltpu.make_async_copy(dir_ref.at[part, :, core_rows, :], dir_s.at[part], in_sems.at[8 + part])
        for part in range(2)
    ]
    small.append(pltpu.make_async_copy(mask_ref.at[core_rows, :], mask_s, in_sems.at[10]))
    pairs = [(part, coil) for part in range(2) for coil in range(4)]
    loads = [
        pltpu.make_async_copy(sens_ref.at[part, coil], sens_s.at[part, coil], in_sems.at[part * 4 + coil])
        for part, coil in pairs
    ]
    stores = [
        pltpu.make_async_copy(
            sens_s.at[part, coil],
            out_ref.at[:, coil // 2, pl.ds((part * 2 + coil % 2) * 32, 32), :],
            out_sems.at[part * 4 + coil],
        )
        for part, coil in pairs
    ]
    stores += [
        pltpu.make_async_copy(small_s, out_ref.at[:, half, pl.ds(128, 48), :], out_sems.at[8 + half])
        for half in range(2)
    ]
    for copy in small + loads:
        copy.start()
    for copy in small:
        copy.wait()
    kept = mask_s[...].astype(jnp.bfloat16)
    for x in range(8):
        for part in range(2):
            small_s[x, pl.ds(part * 16, 16), :] = dir_s[part, x].astype(jnp.bfloat16)
        small_s[x, pl.ds(32, 16), :] = kept
    for copy in stores[8:]:
        copy.start()
    for load, store in zip(loads, stores):
        load.wait()
        store.start()
    for copy in stores:
        copy.wait()


def pack(core, sensitivity, direction, mask_t):
    hbm = pl.BlockSpec(memory_space=pltpu.HBM)
    return pl.pallas_call(
        pack_kernel,
        in_specs=[pl.BlockSpec(memory_space=pltpu.SMEM), hbm, hbm, hbm],
        out_specs=hbm,
        out_shape=jax.ShapeDtypeStruct((8, 2, 176, 512), jnp.bfloat16),
        scratch_shapes=[
            pltpu.VMEM((2, 4, 8, 32, 512), jnp.bfloat16),
            pltpu.VMEM((2, 8, 16, 512), jnp.float32),
            pltpu.VMEM((16, 512), jnp.int32),
            pltpu.VMEM((8, 48, 512), jnp.bfloat16),
            pltpu.SemaphoreType.DMA((11,)),
            pltpu.SemaphoreType.DMA((10,)),
        ],
        compiler_params=pltpu.CompilerParams(vmem_limit_bytes=60 * 1024 * 1024),
        name="pack",
    )(core, sensitivity, direction, mask_t)


def dot(left, right):
    return jnp.dot(left, right, preferred_element_type=jnp.float32)


def spectrum_rows(got_ref, dir_parts, core, fold_ref, image_s, store):
    half = 256
    first_lane = lax.broadcasted_iota(jnp.int32, (half, 128), 1) == 0
    for coil in range(2):
        for yb in range(2):
            cols = pl.ds(yb * half, half)
            dir_re, dir_im = (part[:, :, cols].reshape(half, half).astype(jnp.float32) for part in dir_parts)
            sens_re, sens_im = (
                got_ref[:, pl.ds(pl.multiple_of((part * 2 + coil) * 32 + core * 16, 16), 16), cols]
                .reshape(half, half)
                .astype(jnp.float32)
                for part in range(2)
            )
            image_s[coil, 0, :, cols] = (sens_re * dir_re - sens_im * dir_im).astype(jnp.bfloat16)
            image_s[coil, 1, :, cols] = (sens_re * dir_im + sens_im * dir_re).astype(jnp.bfloat16)
    for coil in range(2):
        from_re = dot(image_s[coil, 0], fold_ref[...])
        from_im = dot(image_s[coil, 1], fold_ref[...])
        re_cos, re_sin = from_re[:, :half], from_re[:, half:]
        im_cos, im_sin = from_im[:, :half], from_im[:, half:]
        low = (re_cos + im_sin, im_cos - re_sin)
        high = (re_cos - im_sin, im_cos + re_sin)
        low_first = (re_cos, im_cos)
        high_first = (re_sin, im_sin)
        for part in range(2):
            for start, value, first in ((0, low[part], low_first[part]), (half, high[part], high_first[part])):
                edge = jnp.where(first_lane, first[:, :128], value[:, :128])
                store(coil, part, start, edge.astype(jnp.bfloat16))
                store(coil, part, start + 128, value[:, 128:].astype(jnp.bfloat16))


def own_rows_kernel(
    coil_ref, got_ref, fold_ref, pick_ref, dir_ref, res_ref, img_ref, out_ref, mask_ref, own_ref, image_s, own_s, sems
):
    core = coil_ref[0] % 2
    own_lanes = pl.ds(pl.multiple_of(coil_ref[0] // 2 * 128, 128), 128)
    own_copies = [
        pltpu.make_async_copy(ref.at[:, :, :, own_lanes], own_s.at[index], sems.at[index])
        for index, ref in enumerate((dir_ref, res_ref, img_ref))
    ]
    for copy in own_copies:
        copy.start()

    def store(coil, part, start, value):
        out_ref[coil, part, :, :, pl.ds(start, 128)] = value.reshape(16, 16, 128)

    dir_parts = [got_ref.at[:, pl.ds(128 + part * 16, 16), :] for part in range(2)]
    spectrum_rows(got_ref, dir_parts, core, fold_ref, image_s, store)
    mask_ref[...] = mask_columns(got_ref[:, pl.ds(160, 16), :], pick_ref)
    for copy in own_copies:
        copy.wait()
    for index in range(3):
        even, odd = paired(*(own_s[index, part].reshape(256, 128) for part in range(2)))
        own_ref[index] = jnp.where(core == 0, even, odd).reshape(8, 32, 128)


def mask_columns(rows, pick_ref):
    return dot(rows.reshape(256, 512), pick_ref[...]).astype(jnp.bfloat16).reshape(16, 16, 512)


def paired(re, im):
    lower = lax.broadcasted_iota(jnp.int32, re.shape, 1) < 64
    moved = pltpu.roll(jnp.where(lower, im, re), 64, 1)
    return jnp.where(lower, re, moved), jnp.where(lower, moved, im)


def own_rows(coil, got, fold, pick, direction, residual, image):
    hbm = pl.BlockSpec(memory_space=pltpu.HBM)
    vmem = pl.BlockSpec(memory_space=pltpu.VMEM)
    return pl.pallas_call(
        own_rows_kernel,
        in_specs=[pl.BlockSpec(memory_space=pltpu.SMEM)] + [vmem] * 3 + [hbm] * 3,
        out_specs=[vmem] * 3,
        out_shape=[
            jax.ShapeDtypeStruct((2, 2, 16, 16, 512), jnp.bfloat16),
            jax.ShapeDtypeStruct((16, 16, 512), jnp.bfloat16),
            jax.ShapeDtypeStruct((3, 8, 32, 128), jnp.float32),
        ],
        scratch_shapes=[
            pltpu.VMEM((2, 2, 256, 512), jnp.bfloat16),
            pltpu.VMEM((3, 2, 8, 32, 128), jnp.float32),
            pltpu.SemaphoreType.DMA((3,)),
        ],
        compiler_params=pltpu.CompilerParams(vmem_limit_bytes=16 * 1024 * 1024),
        name="own_rows",
    )(coil, got, fold, pick, direction, residual, image)


def operator_kernel(
    coil_ref, got_ref, mate_ref, ready_ref, mask_ref, fold_ref, fold_t_ref, pick_ref, pick_t_ref,
    z_back_ref, y_even_ref, y_odd_ref,
    keep_ref, send_ref,
    image_s, spec_s, even_s, odd_s, mask_t_s, mask_s,
):
    size = 512
    half = 256
    f32 = jnp.float32
    bf16 = jnp.bfloat16
    core = coil_ref[0] % 2
    def store(coil, part, start, value):
        spec_s[coil, part, :, 1 - core, :, pl.ds(start, 128)] = value.reshape(16, 16, 128)

    dir_parts = [mate_ref.at[:, pl.ds(part * 16, 16), :] for part in range(2)]
    spectrum_rows(got_ref, dir_parts, 1 - core, fold_ref, image_s, store)
    for coil in range(2):
        for part in range(2):
            spec_s[coil, part, :, core] = ready_ref[coil, part]

    mask_t_s[:, core] = mask_ref[...]
    mask_t_s[:, 1 - core] = mask_columns(mate_ref[:, pl.ds(32, 16), :], pick_ref)
    mask_s[...] = dot(pick_t_ref[...], mask_t_s[...].reshape(size, size)).T

    def sens(coil, part, block, lanes):
        rows = got_ref[pl.ds(block * 8, 8), pl.ds((part * 2 + coil) * 32, 32), lanes]
        return rows.reshape(half, -1).astype(f32)

    first_row = lax.broadcasted_iota(jnp.int32, (64, half), 0) == 0
    for coil in range(2):
        full_re = dot(fold_t_ref[...], spec_s[coil, 0].reshape(size, size))
        full_im = dot(fold_t_ref[...], spec_s[coil, 1].reshape(size, size))
        for nb in range(2):
            cols = pl.ds(nb * half, half)
            from_re = full_re[:, nb * half : nb * half + half]
            from_im = full_im[:, nb * half : nb * half + half]

            def kept(rest):
                pieces = [[], []]
                for side, at in enumerate(QUARTERS[rest]):
                    rows = slice(at * 64, at * 64 + 64)
                    rows_2 = slice(half + at * 64, half + at * 64 + 64)
                    re_cos, re_sin = from_re[rows], from_re[rows_2]
                    im_cos, im_sin = from_im[rows], from_im[rows_2]
                    if side == 0:
                        value, first = (re_cos + im_sin, im_cos - re_sin), (re_cos, im_cos)
                    else:
                        value, first = (re_cos - im_sin, im_cos + re_sin), (re_sin, im_sin)
                    keep = mask_s[rows_2 if side else rows, cols]
                    for part in range(2):
                        piece = jnp.where(first_row, first[part], value[part]) if at == 0 else value[part]
                        pieces[part].append((piece * keep).astype(bf16))
                return jnp.concatenate(pieces[0] + pieces[1], axis=0)

            e0, e1, e2, e3 = (dot(z_back_ref[rest], kept(rest)) for rest in range(4))
            sum_02, dif_02, sum_13, dif_13 = e0 + e2, e0 - e2, e1 + e3, e1 - e3
            turned = (dif_02[:128] - dif_13[128:], dif_02[128:] + dif_13[:128])
            turned_back = (dif_02[:128] + dif_13[128:], dif_02[128:] - dif_13[:128])
            plus, minus = sum_02 + sum_13, sum_02 - sum_13
            quarters = ((plus[:128], plus[128:]), turned, (minus[:128], minus[128:]), turned_back)
            for part in range(2):
                at = pl.ds(part * half + nb * 128, 128)
                for block in range(4):
                    back = quarters[block][part].astype(bf16)
                    even_s[coil, pl.ds(block * 128, 128), at] = back[:, :128]
                    odd_s[coil, pl.ds(block * 128, 128), at] = back[:, 128:]

    for block in range(2):
        rows = pl.ds(block * half, half)
        sums = [[jnp.zeros((half, half), f32) for _ in range(2)] for _ in range(2)]
        for coil in range(2):
            even = dot(even_s[coil, rows, :], y_even_ref[...])
            odd = dot(odd_s[coil, rows, :], y_odd_ref[...])
            for yb in range(2):
                full = even + odd if yb == 0 else even - odd
                re, im = full[:, :half], full[:, half:]
                sens_re, sens_im = (sens(coil, part, block, pl.ds(yb * half, half)) for part in range(2))
                sums[yb][0] += sens_re * re + sens_im * im
                sums[yb][1] += sens_re * im - sens_im * re
        for yb in range(2):
            for lb in range(2):
                lanes = slice(lb * 128, lb * 128 + 128)
                even, odd = paired(sums[yb][0][:, lanes], sums[yb][1][:, lanes])
                slabs = pl.ds(block * 8, 8)
                keep_ref[slabs, yb * 2 + lb] = jnp.where(core == 0, even, odd).reshape(8, 32, 128)
                send_ref[slabs, yb * 2 + lb] = jnp.where(core == 0, odd, even).reshape(8, 32, 128).astype(bf16)


def operator(coil, got, mate, ready, mask, fold_tabs):
    smem = pl.BlockSpec(memory_space=pltpu.SMEM)
    vmem = pl.BlockSpec(memory_space=pltpu.VMEM)
    return pl.pallas_call(
        operator_kernel,
        in_specs=[smem] + [vmem] * 11,
        out_specs=[vmem] * 2,
        out_shape=[
            jax.ShapeDtypeStruct((16, 4, 32, 128), jnp.float32),
            jax.ShapeDtypeStruct((16, 4, 32, 128), jnp.bfloat16),
        ],
        scratch_shapes=[
            pltpu.VMEM((2, 2, 256, 512), jnp.bfloat16),
            pltpu.VMEM((2, 2, 16, 2, 16, 512), jnp.bfloat16),
            pltpu.VMEM((2, 512, 512), jnp.bfloat16),
            pltpu.VMEM((2, 512, 512), jnp.bfloat16),
            pltpu.VMEM((16, 2, 16, 512), jnp.bfloat16),
            pltpu.VMEM((512, 512), jnp.float32),
        ],
        compiler_params=pltpu.CompilerParams(vmem_limit_bytes=32 * 1024 * 1024),
        name="operator",
    )(coil, got, mate, ready, mask, *fold_tabs)


def sums_kernel(part_ref, own_ref, applied_ref, sums_ref):
    def body(x, carry):
        rr, da, ra, aa = carry
        total = jnp.zeros(applied_ref.shape[1:], jnp.float32)
        for coil in range(4):
            for pair in range(2):
                total += part_ref[x, pair, coil].astype(jnp.float32)
        direction = own_ref[0, x]
        residual = own_ref[1, x]
        applied = total + ridge_weight * direction
        applied_ref[x] = applied
        return (
            rr + residual * residual,
            da + direction * applied,
            ra + residual * applied,
            aa + applied * applied,
        )

    zero = jnp.zeros(applied_ref.shape[1:], jnp.float32)
    sums = lax.fori_loop(0, applied_ref.shape[0], body, (zero,) * 4)
    lane = lax.broadcasted_iota(jnp.int32, (1, 128), 1)
    row = jnp.zeros((1, 128), jnp.float32)
    for index, value in enumerate(sums):
        row = jnp.where(lane == index, jnp.sum(value), row)
    sums_ref[...] = jnp.broadcast_to(row, sums_ref.shape)


def final_kernel(all_ref, applied_ref, own_ref, img_out, res_out, dir_out):
    total = jnp.sum(all_ref[...], axis=0, keepdims=True)
    rr, da, ra, aa = (total[:, i : i + 1] for i in range(4))
    step = rr / da
    new = rr + step * (step * aa - 2.0 * ra)
    beta = new / rr
    step = step.reshape(1, 1, 1)
    beta = beta.reshape(1, 1, 1)
    direction = own_ref[0]
    img = own_ref[2] + step * direction
    res = own_ref[1] - step * applied_ref[...]
    nxt = res + beta * direction
    for out, value in ((img_out, img), (res_out, res), (dir_out, nxt)):
        out[0] = value[:, :, :64]
        out[1] = value[:, :, 64:]


def on_device(image, residual, direction, sensitivity, sampling):
    fold_tabs = [jnp.asarray(table) for table in fold_tables(512)]
    coil = lax.axis_index("coil").reshape(1)
    mates = [(at, at ^ 1) for at in range(8)]
    same_core = [[at * 16 + to for to in range(16) for at in range(side, 8, 2)] for side in range(2)]
    packed = pack(coil % 2, sensitivity, direction, sampling.T)
    got = lax.all_to_all(packed.reshape(16, 176, 512), "space", 0, 0, tiled=True)
    mate = lax.ppermute(got[:, 128:], "coil", mates)
    ready, mask, own = own_rows(coil, got, fold_tabs[0], fold_tabs[2], direction, residual, image)
    keep, send = operator(coil, got, mate, ready, mask, fold_tabs)
    pair_sum = (keep + lax.ppermute(send, "coil", mates)).astype(jnp.bfloat16)
    parts = lax.all_to_all(
        pair_sum.reshape(64, 32, 128), ("coil", "space"), 0, 0, axis_index_groups=same_core, tiled=True
    )
    whole = pl.BlockSpec(memory_space=pltpu.VMEM)
    params = pltpu.CompilerParams(vmem_limit_bytes=vmem_limit)
    applied, sums = pl.pallas_call(
        sums_kernel,
        in_specs=[whole] * 2,
        out_specs=[whole] * 2,
        out_shape=[
            jax.ShapeDtypeStruct((8, 32, 128), jnp.float32),
            jax.ShapeDtypeStruct((128, 128), jnp.float32),
        ],
        compiler_params=params,
        name="sums",
    )(parts.reshape(8, 2, 4, 32, 128), own)
    everyone = lax.all_to_all(sums, ("space", "coil"), split_axis=0, concat_axis=0, tiled=True)
    outs = pl.pallas_call(
        final_kernel,
        in_specs=[whole] * 3,
        out_specs=[whole] * 3,
        out_shape=[jax.ShapeDtypeStruct((2, 8, 32, 64), jnp.float32)] * 3,
        compiler_params=params,
        name="final",
    )(everyone, applied, own)
    return tuple(outs)


def solution(mesh):
    placed = (
        P(None, None, "space", None),
        P(None, None, "space", None),
        P(None, None, "space", None),
        P(None, "coil", None, "space", None),
        P(None, "space"),
    )
    return jax.shard_map(
        on_device,
        mesh=mesh,
        in_specs=placed,
        out_specs=(P(None, None, "space", "coil"),) * 3,
        check_vma=False,
    )
```

```python
import math

import jax
import jax.numpy as jnp
import ml_dtypes
import numpy as np
from jax import lax
from jax.experimental import pallas as pl
from jax.experimental.pallas import tpu as pltpu
from jax.sharding import PartitionSpec as P

ridge_weight = 0.1
vmem_limit = 8 * 1024 * 1024


def tables(length):
    counter = np.arange(length, dtype=np.int32)
    product_mod = counter[:, None] * counter[None, :] % length
    phase_angle = product_mod.astype(np.float32) * np.float32(2.0 * math.pi / length)
    norm_scale = np.float32(1.0 / math.sqrt(length))
    return np.cos(phase_angle) * norm_scale, np.sin(phase_angle) * norm_scale


QUARTERS = ((0, 0), (2, 3), (1, 1), (3, 2))


def fold_tables(length):
    cos_t, sin_t = tables(length)
    half = length // 2
    low = np.concatenate([np.arange(rest, half, 4) for rest in (0, 2, 1, 3)])
    high = np.where(low == 0, half, length - low)
    sine = sin_t[:, low].copy()
    sine[:, 0] = cos_t[:, half]
    fold = np.concatenate([cos_t[:, low], sine], axis=1)
    pick = np.eye(length, dtype=np.float32)[:, np.concatenate([low, high])]

    def inverse(rows, at):
        cos_g, sin_g = cos_t[:rows, at], sin_t[:rows, at]
        return np.block([[cos_g, -sin_g], [sin_g, cos_g]])

    quarter = half // 4
    outs = [fold, fold.T, pick, pick.T]
    outs.append(
        np.stack(
            [
                inverse(half // 2, np.concatenate([low[a * quarter :][:quarter], high[b * quarter :][:quarter]]))
                for a, b in QUARTERS
            ]
        )
    )
    for start in (0, half // 2):
        group = slice(start, start + half // 2)
        outs.append(inverse(half, np.concatenate([low[group], high[group]])).T)
    return [np.ascontiguousarray(out).astype(ml_dtypes.bfloat16) for out in outs]


def pack_kernel(core_ref, sens_ref, dir_ref, mask_ref, out_ref, sens_s, dir_s, mask_s, small_s, in_sems, out_sems):
    core_rows = pl.ds(pl.multiple_of(core_ref[0] * 16, 16), 16)
    small = [
        pltpu.make_async_copy(dir_ref.at[part, :, core_rows, :], dir_s.at[part], in_sems.at[8 + part])
        for part in range(2)
    ]
    small.append(pltpu.make_async_copy(mask_ref.at[core_rows, :], mask_s, in_sems.at[10]))
    pairs = [(part, coil) for part in range(2) for coil in range(4)]
    loads = [
        pltpu.make_async_copy(sens_ref.at[part, coil], sens_s.at[part, coil], in_sems.at[part * 4 + coil])
        for part, coil in pairs
    ]
    stores = [
        pltpu.make_async_copy(
            sens_s.at[part, coil],
            out_ref.at[:, coil // 2, pl.ds((part * 2 + coil % 2) * 32, 32), :],
            out_sems.at[part * 4 + coil],
        )
        for part, coil in pairs
    ]
    stores += [
        pltpu.make_async_copy(small_s, out_ref.at[:, half, pl.ds(128, 48), :], out_sems.at[8 + half])
        for half in range(2)
    ]
    for copy in small + loads:
        copy.start()
    for copy in small:
        copy.wait()
    kept = mask_s[...].astype(jnp.bfloat16)
    for x in range(8):
        for part in range(2):
            small_s[x, pl.ds(part * 16, 16), :] = dir_s[part, x].astype(jnp.bfloat16)
        small_s[x, pl.ds(32, 16), :] = kept
    for copy in stores[8:]:
        copy.start()
    for load, store in zip(loads, stores):
        load.wait()
        store.start()
    for copy in stores:
        copy.wait()


def pack(core, sensitivity, direction, mask_t):
    hbm = pl.BlockSpec(memory_space=pltpu.HBM)
    return pl.pallas_call(
        pack_kernel,
        in_specs=[pl.BlockSpec(memory_space=pltpu.SMEM), hbm, hbm, hbm],
        out_specs=hbm,
        out_shape=jax.ShapeDtypeStruct((8, 2, 176, 512), jnp.bfloat16),
        scratch_shapes=[
            pltpu.VMEM((2, 4, 8, 32, 512), jnp.bfloat16),
            pltpu.VMEM((2, 8, 16, 512), jnp.float32),
            pltpu.VMEM((16, 512), jnp.int32),
            pltpu.VMEM((8, 48, 512), jnp.bfloat16),
            pltpu.SemaphoreType.DMA((11,)),
            pltpu.SemaphoreType.DMA((10,)),
        ],
        compiler_params=pltpu.CompilerParams(vmem_limit_bytes=60 * 1024 * 1024),
        name="pack",
    )(core, sensitivity, direction, mask_t)


def dot(left, right):
    return jnp.dot(left, right, preferred_element_type=jnp.float32)


def spectrum_rows(got_ref, dir_parts, core, fold_ref, image_s, store):
    half = 256
    first_lane = lax.broadcasted_iota(jnp.int32, (half, 128), 1) == 0
    for coil in range(2):
        for yb in range(2):
            cols = pl.ds(yb * half, half)
            dir_re, dir_im = (part[:, :, cols].reshape(half, half).astype(jnp.float32) for part in dir_parts)
            sens_re, sens_im = (
                got_ref[:, pl.ds(pl.multiple_of((part * 2 + coil) * 32 + core * 16, 16), 16), cols]
                .reshape(half, half)
                .astype(jnp.float32)
                for part in range(2)
            )
            image_s[coil, 0, :, cols] = (sens_re * dir_re - sens_im * dir_im).astype(jnp.bfloat16)
            image_s[coil, 1, :, cols] = (sens_re * dir_im + sens_im * dir_re).astype(jnp.bfloat16)
    for coil in range(2):
        from_re = dot(image_s[coil, 0], fold_ref[...])
        from_im = dot(image_s[coil, 1], fold_ref[...])
        re_cos, re_sin = from_re[:, :half], from_re[:, half:]
        im_cos, im_sin = from_im[:, :half], from_im[:, half:]
        low = (re_cos + im_sin, im_cos - re_sin)
        high = (re_cos - im_sin, im_cos + re_sin)
        low_first = (re_cos, im_cos)
        high_first = (re_sin, im_sin)
        for part in range(2):
            for start, value, first in ((0, low[part], low_first[part]), (half, high[part], high_first[part])):
                edge = jnp.where(first_lane, first[:, :128], value[:, :128])
                store(coil, part, start, edge.astype(jnp.bfloat16))
                store(coil, part, start + 128, value[:, 128:].astype(jnp.bfloat16))


def own_rows_kernel(
    coil_ref, got_ref, fold_ref, pick_ref, dir_ref, res_ref, img_ref, out_ref, mask_ref, own_ref, image_s, own_s, sems
):
    core = coil_ref[0] % 2
    own_lanes = pl.ds(pl.multiple_of(coil_ref[0] // 2 * 128, 128), 128)
    own_copies = [
        pltpu.make_async_copy(ref.at[:, :, :, own_lanes], own_s.at[index], sems.at[index])
        for index, ref in enumerate((dir_ref, res_ref, img_ref))
    ]
    for copy in own_copies:
        copy.start()

    def store(coil, part, start, value):
        out_ref[coil, part, :, :, pl.ds(start, 128)] = value.reshape(16, 16, 128)

    dir_parts = [got_ref.at[:, pl.ds(128 + part * 16, 16), :] for part in range(2)]
    spectrum_rows(got_ref, dir_parts, core, fold_ref, image_s, store)
    mask_ref[...] = mask_columns(got_ref[:, pl.ds(160, 16), :], pick_ref)
    for copy in own_copies:
        copy.wait()
    for index in range(3):
        even, odd = paired(*(own_s[index, part].reshape(256, 128) for part in range(2)))
        own_ref[index] = jnp.where(core == 0, even, odd).reshape(8, 32, 128)


def mask_columns(rows, pick_ref):
    return dot(rows.reshape(256, 512), pick_ref[...]).astype(jnp.bfloat16).reshape(16, 16, 512)


def paired(re, im):
    lower = lax.broadcasted_iota(jnp.int32, re.shape, 1) < 64
    moved = pltpu.roll(jnp.where(lower, im, re), 64, 1)
    return jnp.where(lower, re, moved), jnp.where(lower, moved, im)


def own_rows(coil, got, fold, pick, direction, residual, image):
    hbm = pl.BlockSpec(memory_space=pltpu.HBM)
    vmem = pl.BlockSpec(memory_space=pltpu.VMEM)
    return pl.pallas_call(
        own_rows_kernel,
        in_specs=[pl.BlockSpec(memory_space=pltpu.SMEM)] + [vmem] * 3 + [hbm] * 3,
        out_specs=[vmem] * 3,
        out_shape=[
            jax.ShapeDtypeStruct((2, 2, 16, 16, 512), jnp.bfloat16),
            jax.ShapeDtypeStruct((16, 16, 512), jnp.bfloat16),
            jax.ShapeDtypeStruct((3, 8, 32, 128), jnp.float32),
        ],
        scratch_shapes=[
            pltpu.VMEM((2, 2, 256, 512), jnp.bfloat16),
            pltpu.VMEM((3, 2, 8, 32, 128), jnp.float32),
            pltpu.SemaphoreType.DMA((3,)),
        ],
        compiler_params=pltpu.CompilerParams(vmem_limit_bytes=16 * 1024 * 1024),
        name="own_rows",
    )(coil, got, fold, pick, direction, residual, image)


def operator_kernel(
    coil_ref, got_ref, mate_ref, ready_ref, mask_ref, fold_ref, fold_t_ref, pick_ref, pick_t_ref,
    z_back_ref, y_even_ref, y_odd_ref,
    keep_ref, send_ref,
    image_s, spec_s, even_s, odd_s, mask_t_s, mask_s,
):
    size = 512
    half = 256
    f32 = jnp.float32
    bf16 = jnp.bfloat16
    core = coil_ref[0] % 2
    def store(coil, part, start, value):
        spec_s[coil, part, :, 1 - core, :, pl.ds(start, 128)] = value.reshape(16, 16, 128)

    dir_parts = [mate_ref.at[:, pl.ds(part * 16, 16), :] for part in range(2)]
    spectrum_rows(got_ref, dir_parts, 1 - core, fold_ref, image_s, store)
    for coil in range(2):
        for part in range(2):
            spec_s[coil, part, :, core] = ready_ref[coil, part]

    mask_t_s[:, core] = mask_ref[...]
    mask_t_s[:, 1 - core] = mask_columns(mate_ref[:, pl.ds(32, 16), :], pick_ref)
    mask_s[...] = dot(pick_t_ref[...], mask_t_s[...].reshape(size, size)).T

    def sens(coil, part, block, lanes):
        rows = got_ref[pl.ds(block * 8, 8), pl.ds((part * 2 + coil) * 32, 32), lanes]
        return rows.reshape(half, -1).astype(f32)

    first_row = lax.broadcasted_iota(jnp.int32, (64, half), 0) == 0
    fulls = [[dot(fold_t_ref[...], spec_s[coil, part].reshape(size, size)) for part in range(2)] for coil in range(2)]
    for coil in range(2):
        full_re, full_im = fulls[coil]
        for nb in range(2):
            cols = pl.ds(nb * half, half)
            from_re = full_re[:, nb * half : nb * half + half]
            from_im = full_im[:, nb * half : nb * half + half]

            def kept(rest):
                pieces = [[], []]
                for side, at in enumerate(QUARTERS[rest]):
                    rows = slice(at * 64, at * 64 + 64)
                    rows_2 = slice(half + at * 64, half + at * 64 + 64)
                    re_cos, re_sin = from_re[rows], from_re[rows_2]
                    im_cos, im_sin = from_im[rows], from_im[rows_2]
                    if side == 0:
                        value, first = (re_cos + im_sin, im_cos - re_sin), (re_cos, im_cos)
                    else:
                        value, first = (re_cos - im_sin, im_cos + re_sin), (re_sin, im_sin)
                    keep = mask_s[rows_2 if side else rows, cols]
                    for part in range(2):
                        piece = jnp.where(first_row, first[part], value[part]) if at == 0 else value[part]
                        pieces[part].append((piece * keep).astype(bf16))
                return jnp.concatenate(pieces[0] + pieces[1], axis=0)

            e0, e1, e2, e3 = (dot(z_back_ref[rest], kept(rest)) for rest in range(4))
            sum_02, dif_02, sum_13, dif_13 = e0 + e2, e0 - e2, e1 + e3, e1 - e3
            turned = (dif_02[:128] - dif_13[128:], dif_02[128:] + dif_13[:128])
            turned_back = (dif_02[:128] + dif_13[128:], dif_02[128:] - dif_13[:128])
            plus, minus = sum_02 + sum_13, sum_02 - sum_13
            quarters = ((plus[:128], plus[128:]), turned, (minus[:128], minus[128:]), turned_back)
            for part in range(2):
                at = pl.ds(part * half + nb * 128, 128)
                for block in range(4):
                    back = quarters[block][part].astype(bf16)
                    even_s[coil, pl.ds(block * 128, 128), at] = back[:, :128]
                    odd_s[coil, pl.ds(block * 128, 128), at] = back[:, 128:]

    wholes = [
        [
            [dot(ref[coil, pl.ds(block * half, half), :], table[...]) for ref, table in ((even_s, y_even_ref), (odd_s, y_odd_ref))]
            for coil in range(2)
        ]
        for block in range(2)
    ]
    for block in range(2):
        sums = [[0.0, 0.0], [0.0, 0.0]]
        for coil in range(2):
            even, odd = wholes[block][coil]
            for yb in range(2):
                full = even + odd if yb == 0 else even - odd
                re, im = full[:, :half], full[:, half:]
                sens_re, sens_im = (sens(coil, part, block, pl.ds(yb * half, half)) for part in range(2))
                sums[yb][0] += sens_re * re + sens_im * im
                sums[yb][1] += sens_re * im - sens_im * re
        for yb in range(2):
            for lb in range(2):
                lanes = slice(lb * 128, lb * 128 + 128)
                even, odd = paired(sums[yb][0][:, lanes], sums[yb][1][:, lanes])
                slabs = pl.ds(block * 8, 8)
                keep_ref[slabs, yb * 2 + lb] = jnp.where(core == 0, even, odd).reshape(8, 32, 128)
                send_ref[slabs, yb * 2 + lb] = jnp.where(core == 0, odd, even).reshape(8, 32, 128).astype(bf16)


def operator(coil, got, mate, ready, mask, fold_tabs):
    smem = pl.BlockSpec(memory_space=pltpu.SMEM)
    vmem = pl.BlockSpec(memory_space=pltpu.VMEM)
    return pl.pallas_call(
        operator_kernel,
        in_specs=[smem] + [vmem] * 11,
        out_specs=[vmem] * 2,
        out_shape=[
            jax.ShapeDtypeStruct((16, 4, 32, 128), jnp.float32),
            jax.ShapeDtypeStruct((16, 4, 32, 128), jnp.bfloat16),
        ],
        scratch_shapes=[
            pltpu.VMEM((2, 2, 256, 512), jnp.bfloat16),
            pltpu.VMEM((2, 2, 16, 2, 16, 512), jnp.bfloat16),
            pltpu.VMEM((2, 512, 512), jnp.bfloat16),
            pltpu.VMEM((2, 512, 512), jnp.bfloat16),
            pltpu.VMEM((16, 2, 16, 512), jnp.bfloat16),
            pltpu.VMEM((512, 512), jnp.float32),
        ],
        compiler_params=pltpu.CompilerParams(vmem_limit_bytes=32 * 1024 * 1024),
        name="operator",
    )(coil, got, mate, ready, mask, *fold_tabs)


def sums_kernel(part_ref, own_ref, applied_ref, sums_ref):
    def body(x, carry):
        rr, da, ra, aa = carry
        total = jnp.zeros(applied_ref.shape[1:], jnp.float32)
        for coil in range(4):
            for pair in range(2):
                total += part_ref[x, pair, coil].astype(jnp.float32)
        direction = own_ref[0, x]
        residual = own_ref[1, x]
        applied = total + ridge_weight * direction
        applied_ref[x] = applied
        return (
            rr + residual * residual,
            da + direction * applied,
            ra + residual * applied,
            aa + applied * applied,
        )

    zero = jnp.zeros(applied_ref.shape[1:], jnp.float32)
    sums = lax.fori_loop(0, applied_ref.shape[0], body, (zero,) * 4)
    lane = lax.broadcasted_iota(jnp.int32, (1, 128), 1)
    row = jnp.zeros((1, 128), jnp.float32)
    for index, value in enumerate(sums):
        row = jnp.where(lane == index, jnp.sum(value), row)
    sums_ref[...] = jnp.broadcast_to(row, sums_ref.shape)


def final_kernel(all_ref, applied_ref, own_ref, img_out, res_out, dir_out):
    total = jnp.sum(all_ref[...], axis=0, keepdims=True)
    rr, da, ra, aa = (total[:, i : i + 1] for i in range(4))
    step = rr / da
    new = rr + step * (step * aa - 2.0 * ra)
    beta = new / rr
    step = step.reshape(1, 1, 1)
    beta = beta.reshape(1, 1, 1)
    direction = own_ref[0]
    img = own_ref[2] + step * direction
    res = own_ref[1] - step * applied_ref[...]
    nxt = res + beta * direction
    for out, value in ((img_out, img), (res_out, res), (dir_out, nxt)):
        out[0] = value[:, :, :64]
        out[1] = value[:, :, 64:]


def on_device(image, residual, direction, sensitivity, sampling):
    fold_tabs = [jnp.asarray(table) for table in fold_tables(512)]
    coil = lax.axis_index("coil").reshape(1)
    mates = [(at, at ^ 1) for at in range(8)]
    same_core = [[at * 16 + to for to in range(16) for at in range(side, 8, 2)] for side in range(2)]
    packed = pack(coil % 2, sensitivity, direction, sampling.T)
    got = lax.all_to_all(packed.reshape(16, 176, 512), "space", 0, 0, tiled=True)
    mate = lax.ppermute(got[:, 128:], "coil", mates)
    ready, mask, own = own_rows(coil, got, fold_tabs[0], fold_tabs[2], direction, residual, image)
    keep, send = operator(coil, got, mate, ready, mask, fold_tabs)
    pair_sum = (keep + lax.ppermute(send, "coil", mates)).astype(jnp.bfloat16)
    parts = lax.all_to_all(
        pair_sum.reshape(64, 32, 128), ("coil", "space"), 0, 0, axis_index_groups=same_core, tiled=True
    )
    whole = pl.BlockSpec(memory_space=pltpu.VMEM)
    params = pltpu.CompilerParams(vmem_limit_bytes=vmem_limit)
    applied, sums = pl.pallas_call(
        sums_kernel,
        in_specs=[whole] * 2,
        out_specs=[whole] * 2,
        out_shape=[
            jax.ShapeDtypeStruct((8, 32, 128), jnp.float32),
            jax.ShapeDtypeStruct((128, 128), jnp.float32),
        ],
        compiler_params=params,
        name="sums",
    )(parts.reshape(8, 2, 4, 32, 128), own)
    everyone = lax.all_to_all(sums, ("space", "coil"), split_axis=0, concat_axis=0, tiled=True)
    outs = pl.pallas_call(
        final_kernel,
        in_specs=[whole] * 3,
        out_specs=[whole] * 3,
        out_shape=[jax.ShapeDtypeStruct((2, 8, 32, 64), jnp.float32)] * 3,
        compiler_params=params,
        name="final",
    )(everyone, applied, own)
    return tuple(outs)


def solution(mesh):
    placed = (
        P(None, None, "space", None),
        P(None, None, "space", None),
        P(None, None, "space", None),
        P(None, "coil", None, "space", None),
        P(None, "space"),
    )
    return jax.shard_map(
        on_device,
        mesh=mesh,
        in_specs=placed,
        out_specs=(P(None, None, "space", "coil"),) * 3,
        check_vma=False,
    )
```

```python
import math

import jax
import jax.numpy as jnp
import ml_dtypes
import numpy as np
from jax import lax
from jax.experimental import pallas as pl
from jax.experimental.pallas import tpu as pltpu
from jax.sharding import PartitionSpec as P

ridge_weight = 0.1
vmem_limit = 8 * 1024 * 1024


def tables(length):
    counter = np.arange(length, dtype=np.int32)
    product_mod = counter[:, None] * counter[None, :] % length
    phase_angle = product_mod.astype(np.float32) * np.float32(2.0 * math.pi / length)
    norm_scale = np.float32(1.0 / math.sqrt(length))
    return np.cos(phase_angle) * norm_scale, np.sin(phase_angle) * norm_scale


QUARTERS = ((0, 0), (2, 3), (1, 1), (3, 2))


def fold_tables(length):
    cos_t, sin_t = tables(length)
    half = length // 2
    low = np.concatenate([np.arange(rest, half, 4) for rest in (0, 2, 1, 3)])
    high = np.where(low == 0, half, length - low)
    sine = sin_t[:, low].copy()
    sine[:, 0] = cos_t[:, half]
    fold = np.concatenate([cos_t[:, low], sine], axis=1)
    pick = np.eye(length, dtype=np.float32)[:, np.concatenate([low, high])]

    def inverse(rows, at):
        cos_g, sin_g = cos_t[:rows, at], sin_t[:rows, at]
        return np.block([[cos_g, -sin_g], [sin_g, cos_g]])

    quarter = half // 4
    by_core = fold.T.reshape(length, 16, 2, 16).transpose(2, 0, 1, 3).reshape(2, length, half)
    outs = [fold, by_core, pick, pick.T]
    outs.append(
        np.stack(
            [
                inverse(half // 2, np.concatenate([low[a * quarter :][:quarter], high[b * quarter :][:quarter]]))
                for a, b in QUARTERS
            ]
        )
    )
    for start in (0, half // 2):
        group = slice(start, start + half // 2)
        outs.append(inverse(half, np.concatenate([low[group], high[group]])).T)
    return [np.ascontiguousarray(out).astype(ml_dtypes.bfloat16) for out in outs]


def pack_kernel(core_ref, sens_ref, dir_ref, mask_ref, out_ref, sens_s, dir_s, mask_s, small_s, in_sems, out_sems):
    core_rows = pl.ds(pl.multiple_of(core_ref[0] * 16, 16), 16)
    small = [
        pltpu.make_async_copy(dir_ref.at[part, :, core_rows, :], dir_s.at[part], in_sems.at[8 + part])
        for part in range(2)
    ]
    small.append(pltpu.make_async_copy(mask_ref.at[core_rows, :], mask_s, in_sems.at[10]))
    pairs = [(part, coil) for part in range(2) for coil in range(4)]
    loads = [
        pltpu.make_async_copy(sens_ref.at[part, coil], sens_s.at[part, coil], in_sems.at[part * 4 + coil])
        for part, coil in pairs
    ]
    stores = [
        pltpu.make_async_copy(
            sens_s.at[part, coil],
            out_ref.at[:, coil // 2, pl.ds((part * 2 + coil % 2) * 32, 32), :],
            out_sems.at[part * 4 + coil],
        )
        for part, coil in pairs
    ]
    stores += [
        pltpu.make_async_copy(small_s, out_ref.at[:, half, pl.ds(128, 48), :], out_sems.at[8 + half])
        for half in range(2)
    ]
    for copy in small + loads:
        copy.start()
    for copy in small:
        copy.wait()
    kept = mask_s[...].astype(jnp.bfloat16)
    for x in range(8):
        for part in range(2):
            small_s[x, pl.ds(part * 16, 16), :] = dir_s[part, x].astype(jnp.bfloat16)
        small_s[x, pl.ds(32, 16), :] = kept
    for copy in stores[8:]:
        copy.start()
    for load, store in zip(loads, stores):
        load.wait()
        store.start()
    for copy in stores:
        copy.wait()


def pack(core, sensitivity, direction, mask_t):
    hbm = pl.BlockSpec(memory_space=pltpu.HBM)
    return pl.pallas_call(
        pack_kernel,
        in_specs=[pl.BlockSpec(memory_space=pltpu.SMEM), hbm, hbm, hbm],
        out_specs=hbm,
        out_shape=jax.ShapeDtypeStruct((8, 2, 176, 512), jnp.bfloat16),
        scratch_shapes=[
            pltpu.VMEM((2, 4, 8, 32, 512), jnp.bfloat16),
            pltpu.VMEM((2, 8, 16, 512), jnp.float32),
            pltpu.VMEM((16, 512), jnp.int32),
            pltpu.VMEM((8, 48, 512), jnp.bfloat16),
            pltpu.SemaphoreType.DMA((11,)),
            pltpu.SemaphoreType.DMA((10,)),
        ],
        compiler_params=pltpu.CompilerParams(vmem_limit_bytes=60 * 1024 * 1024),
        name="pack",
    )(core, sensitivity, direction, mask_t)


def dot(left, right):
    return jnp.dot(left, right, preferred_element_type=jnp.float32)


def spectrum_rows(got_ref, dir_parts, core, fold_ref, image_s, store):
    half = 256
    first_lane = lax.broadcasted_iota(jnp.int32, (half, 128), 1) == 0
    for coil in range(2):
        for yb in range(2):
            cols = pl.ds(yb * half, half)
            dir_re, dir_im = (part[:, :, cols].reshape(half, half).astype(jnp.float32) for part in dir_parts)
            sens_re, sens_im = (
                got_ref[:, pl.ds(pl.multiple_of((part * 2 + coil) * 32 + core * 16, 16), 16), cols]
                .reshape(half, half)
                .astype(jnp.float32)
                for part in range(2)
            )
            image_s[coil, 0, :, cols] = (sens_re * dir_re - sens_im * dir_im).astype(jnp.bfloat16)
            image_s[coil, 1, :, cols] = (sens_re * dir_im + sens_im * dir_re).astype(jnp.bfloat16)
    for coil in range(2):
        from_re = dot(image_s[coil, 0], fold_ref[...])
        from_im = dot(image_s[coil, 1], fold_ref[...])
        re_cos, re_sin = from_re[:, :half], from_re[:, half:]
        im_cos, im_sin = from_im[:, :half], from_im[:, half:]
        low = (re_cos + im_sin, im_cos - re_sin)
        high = (re_cos - im_sin, im_cos + re_sin)
        low_first = (re_cos, im_cos)
        high_first = (re_sin, im_sin)
        for part in range(2):
            for start, value, first in ((0, low[part], low_first[part]), (half, high[part], high_first[part])):
                edge = jnp.where(first_lane, first[:, :128], value[:, :128])
                store(coil, part, start, edge.astype(jnp.bfloat16))
                store(coil, part, start + 128, value[:, 128:].astype(jnp.bfloat16))


def own_rows_kernel(
    coil_ref, got_ref, fold_ref, fold_t_ref, pick_ref, dir_ref, res_ref, img_ref,
    share_ref, mask_ref, own_ref,
    image_s, spec_s, own_s, sems,
):
    core = coil_ref[0] % 2
    own_lanes = pl.ds(pl.multiple_of(coil_ref[0] // 2 * 128, 128), 128)
    own_copies = [
        pltpu.make_async_copy(ref.at[:, :, :, own_lanes], own_s.at[index], sems.at[index])
        for index, ref in enumerate((dir_ref, res_ref, img_ref))
    ]
    for copy in own_copies:
        copy.start()

    def store(coil, part, start, value):
        spec_s[coil, part, :, pl.ds(start, 128)] = value

    dir_parts = [got_ref.at[:, pl.ds(128 + part * 16, 16), :] for part in range(2)]
    spectrum_rows(got_ref, dir_parts, core, fold_ref, image_s, store)
    mask_ref[...] = mask_columns(got_ref[:, pl.ds(160, 16), :], pick_ref)
    for coil in range(2):
        for part in range(2):
            share_ref[coil, part] = dot(fold_t_ref[core], spec_s[coil, part])
    for copy in own_copies:
        copy.wait()
    for index in range(3):
        even, odd = paired(*(own_s[index, part].reshape(256, 128) for part in range(2)))
        own_ref[index] = jnp.where(core == 0, even, odd).reshape(8, 32, 128)


def mask_columns(rows, pick_ref):
    return dot(rows.reshape(256, 512), pick_ref[...]).astype(jnp.bfloat16).reshape(16, 16, 512)


def paired(re, im):
    lower = lax.broadcasted_iota(jnp.int32, re.shape, 1) < 64
    moved = pltpu.roll(jnp.where(lower, im, re), 64, 1)
    return jnp.where(lower, re, moved), jnp.where(lower, moved, im)


def own_rows(coil, got, fold, fold_t, pick, direction, residual, image):
    hbm = pl.BlockSpec(memory_space=pltpu.HBM)
    vmem = pl.BlockSpec(memory_space=pltpu.VMEM)
    return pl.pallas_call(
        own_rows_kernel,
        in_specs=[pl.BlockSpec(memory_space=pltpu.SMEM)] + [vmem] * 4 + [hbm] * 3,
        out_specs=[vmem] * 3,
        out_shape=[
            jax.ShapeDtypeStruct((2, 2, 512, 512), jnp.float32),
            jax.ShapeDtypeStruct((16, 16, 512), jnp.bfloat16),
            jax.ShapeDtypeStruct((3, 8, 32, 128), jnp.float32),
        ],
        scratch_shapes=[
            pltpu.VMEM((2, 2, 256, 512), jnp.bfloat16),
            pltpu.VMEM((2, 2, 256, 512), jnp.bfloat16),
            pltpu.VMEM((3, 2, 8, 32, 128), jnp.float32),
            pltpu.SemaphoreType.DMA((3,)),
        ],
        compiler_params=pltpu.CompilerParams(vmem_limit_bytes=16 * 1024 * 1024),
        name="own_rows",
    )(coil, got, fold, fold_t, pick, direction, residual, image)


def operator_kernel(
    coil_ref, got_ref, mate_ref, share_ref, mask_ref, fold_ref, fold_t_ref, pick_ref, pick_t_ref,
    z_back_ref, y_even_ref, y_odd_ref,
    keep_ref, send_ref,
    image_s, spec_s, even_s, odd_s, mask_t_s, mask_s,
):
    size = 512
    half = 256
    f32 = jnp.float32
    bf16 = jnp.bfloat16
    core = coil_ref[0] % 2
    def store(coil, part, start, value):
        spec_s[coil, part, :, pl.ds(start, 128)] = value

    dir_parts = [mate_ref.at[:, pl.ds(part * 16, 16), :] for part in range(2)]
    spectrum_rows(got_ref, dir_parts, 1 - core, fold_ref, image_s, store)

    mask_t_s[:, core] = mask_ref[...]
    mask_t_s[:, 1 - core] = mask_columns(mate_ref[:, pl.ds(32, 16), :], pick_ref)
    mask_s[...] = dot(pick_t_ref[...], mask_t_s[...].reshape(size, size)).T

    def sens(coil, part, block, lanes):
        rows = got_ref[pl.ds(block * 8, 8), pl.ds((part * 2 + coil) * 32, 32), lanes]
        return rows.reshape(half, -1).astype(f32)

    first_row = lax.broadcasted_iota(jnp.int32, (64, half), 0) == 0
    fulls = [
        [share_ref[coil, part] + dot(fold_t_ref[1 - core], spec_s[coil, part]) for part in range(2)] for coil in range(2)
    ]
    for coil in range(2):
        full_re, full_im = fulls[coil]
        for nb in range(2):
            cols = pl.ds(nb * half, half)
            from_re = full_re[:, nb * half : nb * half + half]
            from_im = full_im[:, nb * half : nb * half + half]

            def kept(rest):
                pieces = [[], []]
                for side, at in enumerate(QUARTERS[rest]):
                    rows = slice(at * 64, at * 64 + 64)
                    rows_2 = slice(half + at * 64, half + at * 64 + 64)
                    re_cos, re_sin = from_re[rows], from_re[rows_2]
                    im_cos, im_sin = from_im[rows], from_im[rows_2]
                    if side == 0:
                        value, first = (re_cos + im_sin, im_cos - re_sin), (re_cos, im_cos)
                    else:
                        value, first = (re_cos - im_sin, im_cos + re_sin), (re_sin, im_sin)
                    keep = mask_s[rows_2 if side else rows, cols]
                    for part in range(2):
                        piece = jnp.where(first_row, first[part], value[part]) if at == 0 else value[part]
                        pieces[part].append((piece * keep).astype(bf16))
                return jnp.concatenate(pieces[0] + pieces[1], axis=0)

            e0, e1, e2, e3 = (dot(z_back_ref[rest], kept(rest)) for rest in range(4))
            sum_02, dif_02, sum_13, dif_13 = e0 + e2, e0 - e2, e1 + e3, e1 - e3
            turned = (dif_02[:128] - dif_13[128:], dif_02[128:] + dif_13[:128])
            turned_back = (dif_02[:128] + dif_13[128:], dif_02[128:] - dif_13[:128])
            plus, minus = sum_02 + sum_13, sum_02 - sum_13
            quarters = ((plus[:128], plus[128:]), turned, (minus[:128], minus[128:]), turned_back)
            for part in range(2):
                at = pl.ds(part * half + nb * 128, 128)
                for block in range(4):
                    back = quarters[block][part].astype(bf16)
                    even_s[coil, pl.ds(block * 128, 128), at] = back[:, :128]
                    odd_s[coil, pl.ds(block * 128, 128), at] = back[:, 128:]

    wholes = [
        [
            [dot(ref[coil, pl.ds(block * half, half), :], table[...]) for ref, table in ((even_s, y_even_ref), (odd_s, y_odd_ref))]
            for coil in range(2)
        ]
        for block in range(2)
    ]
    for block in range(2):
        sums = [[0.0, 0.0], [0.0, 0.0]]
        for coil in range(2):
            even, odd = wholes[block][coil]
            for yb in range(2):
                full = even + odd if yb == 0 else even - odd
                re, im = full[:, :half], full[:, half:]
                sens_re, sens_im = (sens(coil, part, block, pl.ds(yb * half, half)) for part in range(2))
                sums[yb][0] += sens_re * re + sens_im * im
                sums[yb][1] += sens_re * im - sens_im * re
        for yb in range(2):
            for lb in range(2):
                lanes = slice(lb * 128, lb * 128 + 128)
                even, odd = paired(sums[yb][0][:, lanes], sums[yb][1][:, lanes])
                slabs = pl.ds(block * 8, 8)
                keep_ref[slabs, yb * 2 + lb] = jnp.where(core == 0, even, odd).reshape(8, 32, 128)
                send_ref[slabs, yb * 2 + lb] = jnp.where(core == 0, odd, even).reshape(8, 32, 128).astype(bf16)


def operator(coil, got, mate, share, mask, fold_tabs):
    smem = pl.BlockSpec(memory_space=pltpu.SMEM)
    vmem = pl.BlockSpec(memory_space=pltpu.VMEM)
    return pl.pallas_call(
        operator_kernel,
        in_specs=[smem] + [vmem] * 11,
        out_specs=[vmem] * 2,
        out_shape=[
            jax.ShapeDtypeStruct((16, 4, 32, 128), jnp.float32),
            jax.ShapeDtypeStruct((16, 4, 32, 128), jnp.bfloat16),
        ],
        scratch_shapes=[
            pltpu.VMEM((2, 2, 256, 512), jnp.bfloat16),
            pltpu.VMEM((2, 2, 256, 512), jnp.bfloat16),
            pltpu.VMEM((2, 512, 512), jnp.bfloat16),
            pltpu.VMEM((2, 512, 512), jnp.bfloat16),
            pltpu.VMEM((16, 2, 16, 512), jnp.bfloat16),
            pltpu.VMEM((512, 512), jnp.float32),
        ],
        compiler_params=pltpu.CompilerParams(vmem_limit_bytes=32 * 1024 * 1024),
        name="operator",
    )(coil, got, mate, share, mask, *fold_tabs)


def sums_kernel(part_ref, own_ref, applied_ref, sums_ref):
    def body(x, carry):
        rr, da, ra, aa = carry
        total = jnp.zeros(applied_ref.shape[1:], jnp.float32)
        for coil in range(4):
            for pair in range(2):
                total += part_ref[x, pair, coil].astype(jnp.float32)
        direction = own_ref[0, x]
        residual = own_ref[1, x]
        applied = total + ridge_weight * direction
        applied_ref[x] = applied
        return (
            rr + residual * residual,
            da + direction * applied,
            ra + residual * applied,
            aa + applied * applied,
        )

    zero = jnp.zeros(applied_ref.shape[1:], jnp.float32)
    sums = lax.fori_loop(0, applied_ref.shape[0], body, (zero,) * 4)
    lane = lax.broadcasted_iota(jnp.int32, (1, 128), 1)
    row = jnp.zeros((1, 128), jnp.float32)
    for index, value in enumerate(sums):
        row = jnp.where(lane == index, jnp.sum(value), row)
    sums_ref[...] = jnp.broadcast_to(row, sums_ref.shape)


def final_kernel(all_ref, applied_ref, own_ref, img_out, res_out, dir_out):
    total = jnp.sum(all_ref[...], axis=0, keepdims=True)
    rr, da, ra, aa = (total[:, i : i + 1] for i in range(4))
    step = rr / da
    new = rr + step * (step * aa - 2.0 * ra)
    beta = new / rr
    step = step.reshape(1, 1, 1)
    beta = beta.reshape(1, 1, 1)
    direction = own_ref[0]
    img = own_ref[2] + step * direction
    res = own_ref[1] - step * applied_ref[...]
    nxt = res + beta * direction
    for out, value in ((img_out, img), (res_out, res), (dir_out, nxt)):
        out[0] = value[:, :, :64]
        out[1] = value[:, :, 64:]


def on_device(image, residual, direction, sensitivity, sampling):
    fold_tabs = [jnp.asarray(table) for table in fold_tables(512)]
    coil = lax.axis_index("coil").reshape(1)
    mates = [(at, at ^ 1) for at in range(8)]
    same_core = [[at * 16 + to for to in range(16) for at in range(side, 8, 2)] for side in range(2)]
    packed = pack(coil % 2, sensitivity, direction, sampling.T)
    got = lax.all_to_all(packed.reshape(16, 176, 512), "space", 0, 0, tiled=True)
    mate = lax.ppermute(got[:, 128:], "coil", mates)
    share, mask, own = own_rows(coil, got, *fold_tabs[:3], direction, residual, image)
    keep, send = operator(coil, got, mate, share, mask, fold_tabs)
    pair_sum = (keep + lax.ppermute(send, "coil", mates)).astype(jnp.bfloat16)
    parts = lax.all_to_all(
        pair_sum.reshape(64, 32, 128), ("coil", "space"), 0, 0, axis_index_groups=same_core, tiled=True
    )
    whole = pl.BlockSpec(memory_space=pltpu.VMEM)
    params = pltpu.CompilerParams(vmem_limit_bytes=vmem_limit)
    applied, sums = pl.pallas_call(
        sums_kernel,
        in_specs=[whole] * 2,
        out_specs=[whole] * 2,
        out_shape=[
            jax.ShapeDtypeStruct((8, 32, 128), jnp.float32),
            jax.ShapeDtypeStruct((128, 128), jnp.float32),
        ],
        compiler_params=params,
        name="sums",
    )(parts.reshape(8, 2, 4, 32, 128), own)
    everyone = lax.all_to_all(sums, ("space", "coil"), split_axis=0, concat_axis=0, tiled=True)
    outs = pl.pallas_call(
        final_kernel,
        in_specs=[whole] * 3,
        out_specs=[whole] * 3,
        out_shape=[jax.ShapeDtypeStruct((2, 8, 32, 64), jnp.float32)] * 3,
        compiler_params=params,
        name="final",
    )(everyone, applied, own)
    return tuple(outs)


def solution(mesh):
    placed = (
        P(None, None, "space", None),
        P(None, None, "space", None),
        P(None, None, "space", None),
        P(None, "coil", None, "space", None),
        P(None, "space"),
    )
    return jax.shard_map(
        on_device,
        mesh=mesh,
        in_specs=placed,
        out_specs=(P(None, None, "space", "coil"),) * 3,
        check_vma=False,
    )
```

```python
import math

import jax
import jax.numpy as jnp
import ml_dtypes
import numpy as np
from jax import lax
from jax.experimental import pallas as pl
from jax.experimental.pallas import tpu as pltpu
from jax.sharding import PartitionSpec as P

ridge_weight = 0.1
vmem_limit = 8 * 1024 * 1024


def tables(length):
    counter = np.arange(length, dtype=np.int32)
    product_mod = counter[:, None] * counter[None, :] % length
    phase_angle = product_mod.astype(np.float32) * np.float32(2.0 * math.pi / length)
    norm_scale = np.float32(1.0 / math.sqrt(length))
    return np.cos(phase_angle) * norm_scale, np.sin(phase_angle) * norm_scale


QUARTERS = ((0, 0), (2, 3), (1, 1), (3, 2))


def fold_tables(length):
    cos_t, sin_t = tables(length)
    half = length // 2
    low = np.concatenate([np.arange(rest, half, 4) for rest in (0, 2, 1, 3)])
    high = np.where(low == 0, half, length - low)
    sine = sin_t[:, low].copy()
    sine[:, 0] = cos_t[:, half]
    fold = np.concatenate([cos_t[:, low], sine], axis=1)
    pick = np.eye(length, dtype=np.float32)[:, np.concatenate([low, high])]

    def inverse(rows, at):
        cos_g, sin_g = cos_t[:rows, at], sin_t[:rows, at]
        return np.block([[cos_g, -sin_g], [sin_g, cos_g]])

    quarter = half // 4
    by_core = fold.T.reshape(length, 16, 2, 16).transpose(2, 0, 1, 3).reshape(2, length, half)
    outs = [fold, by_core, pick, pick.T]
    outs.append(
        np.stack(
            [
                inverse(half // 2, np.concatenate([low[a * quarter :][:quarter], high[b * quarter :][:quarter]]))
                for a, b in QUARTERS
            ]
        )
    )
    for start in (0, half // 2):
        group = slice(start, start + half // 2)
        outs.append(inverse(half, np.concatenate([low[group], high[group]])).T)
    return [np.ascontiguousarray(out).astype(ml_dtypes.bfloat16) for out in outs]


def pack_kernel(core_ref, sens_ref, dir_ref, mask_ref, out_ref, sens_s, dir_s, mask_s, small_s, in_sems, out_sems):
    core_rows = pl.ds(pl.multiple_of(core_ref[0] * 16, 16), 16)
    small = [
        pltpu.make_async_copy(dir_ref.at[part, :, core_rows, :], dir_s.at[part], in_sems.at[8 + part])
        for part in range(2)
    ]
    small.append(pltpu.make_async_copy(mask_ref.at[core_rows, :], mask_s, in_sems.at[10]))
    pairs = [(part, coil) for part in range(2) for coil in range(4)]
    loads = [
        pltpu.make_async_copy(sens_ref.at[part, coil], sens_s.at[part, coil], in_sems.at[part * 4 + coil])
        for part, coil in pairs
    ]
    stores = [
        pltpu.make_async_copy(
            sens_s.at[part, coil],
            out_ref.at[:, coil // 2, pl.ds((part * 2 + coil % 2) * 32, 32), :],
            out_sems.at[part * 4 + coil],
        )
        for part, coil in pairs
    ]
    stores += [
        pltpu.make_async_copy(small_s, out_ref.at[:, half, pl.ds(128, 48), :], out_sems.at[8 + half])
        for half in range(2)
    ]
    for copy in small + loads:
        copy.start()
    for copy in small:
        copy.wait()
    kept = mask_s[...].astype(jnp.bfloat16)
    for x in range(8):
        for part in range(2):
            small_s[x, pl.ds(part * 16, 16), :] = dir_s[part, x].astype(jnp.bfloat16)
        small_s[x, pl.ds(32, 16), :] = kept
    for copy in stores[8:]:
        copy.start()
    for load, store in zip(loads, stores):
        load.wait()
        store.start()
    for copy in stores:
        copy.wait()


def pack(core, sensitivity, direction, mask_t):
    hbm = pl.BlockSpec(memory_space=pltpu.HBM)
    return pl.pallas_call(
        pack_kernel,
        in_specs=[pl.BlockSpec(memory_space=pltpu.SMEM), hbm, hbm, hbm],
        out_specs=hbm,
        out_shape=jax.ShapeDtypeStruct((8, 2, 176, 512), jnp.bfloat16),
        scratch_shapes=[
            pltpu.VMEM((2, 4, 8, 32, 512), jnp.bfloat16),
            pltpu.VMEM((2, 8, 16, 512), jnp.float32),
            pltpu.VMEM((16, 512), jnp.int32),
            pltpu.VMEM((8, 48, 512), jnp.bfloat16),
            pltpu.SemaphoreType.DMA((11,)),
            pltpu.SemaphoreType.DMA((10,)),
        ],
        compiler_params=pltpu.CompilerParams(vmem_limit_bytes=60 * 1024 * 1024),
        name="pack",
    )(core, sensitivity, direction, mask_t)


def dot(left, right):
    return jnp.dot(left, right, preferred_element_type=jnp.float32)


def spectrum_rows(got_ref, dir_parts, core, fold_ref, image_s, store):
    half = 256
    first_lane = lax.broadcasted_iota(jnp.int32, (half, 128), 1) == 0
    for coil in range(2):
        for yb in range(2):
            cols = pl.ds(yb * half, half)
            dir_re, dir_im = (part[:, :, cols].reshape(half, half).astype(jnp.float32) for part in dir_parts)
            sens_re, sens_im = (
                got_ref[:, pl.ds(pl.multiple_of((part * 2 + coil) * 32 + core * 16, 16), 16), cols]
                .reshape(half, half)
                .astype(jnp.float32)
                for part in range(2)
            )
            image_s[coil, 0, :, cols] = (sens_re * dir_re - sens_im * dir_im).astype(jnp.bfloat16)
            image_s[coil, 1, :, cols] = (sens_re * dir_im + sens_im * dir_re).astype(jnp.bfloat16)
    for coil in range(2):
        from_re = dot(image_s[coil, 0], fold_ref[...])
        from_im = dot(image_s[coil, 1], fold_ref[...])
        re_cos, re_sin = from_re[:, :half], from_re[:, half:]
        im_cos, im_sin = from_im[:, :half], from_im[:, half:]
        low = (re_cos + im_sin, im_cos - re_sin)
        high = (re_cos - im_sin, im_cos + re_sin)
        low_first = (re_cos, im_cos)
        high_first = (re_sin, im_sin)
        for part in range(2):
            for start, value, first in ((0, low[part], low_first[part]), (half, high[part], high_first[part])):
                edge = jnp.where(first_lane, first[:, :128], value[:, :128])
                store(coil, part, start, edge.astype(jnp.bfloat16))
                store(coil, part, start + 128, value[:, 128:].astype(jnp.bfloat16))


def own_rows_kernel(
    coil_ref, got_ref, fold_ref, fold_t_ref, pick_ref, dir_ref, res_ref, img_ref,
    share_ref, mask_ref, own_ref,
    image_s, spec_s, own_s, sems,
):
    core = coil_ref[0] % 2
    own_lanes = pl.ds(pl.multiple_of(coil_ref[0] // 2 * 128, 128), 128)
    own_copies = [
        pltpu.make_async_copy(ref.at[:, :, :, own_lanes], own_s.at[index], sems.at[index])
        for index, ref in enumerate((dir_ref, res_ref, img_ref))
    ]
    for copy in own_copies:
        copy.start()

    def store(coil, part, start, value):
        spec_s[coil, part, :, pl.ds(start, 128)] = value

    dir_parts = [got_ref.at[:, pl.ds(128 + part * 16, 16), :] for part in range(2)]
    spectrum_rows(got_ref, dir_parts, core, fold_ref, image_s, store)
    mask_ref[...] = mask_columns(got_ref[:, pl.ds(160, 16), :], pick_ref)
    for coil in range(2):
        for part in range(2):
            share_ref[coil, part] = dot(fold_t_ref[core], spec_s[coil, part])
    for copy in own_copies:
        copy.wait()
    for index in range(3):
        even, odd = paired(*(own_s[index, part].reshape(256, 128) for part in range(2)))
        own_ref[index] = jnp.where(core == 0, even, odd).reshape(8, 32, 128)


def mask_columns(rows, pick_ref):
    return dot(rows.reshape(256, 512), pick_ref[...]).astype(jnp.bfloat16).reshape(16, 16, 512)


def paired(re, im):
    lower = lax.broadcasted_iota(jnp.int32, re.shape, 1) < 64
    moved = pltpu.roll(jnp.where(lower, im, re), 64, 1)
    return jnp.where(lower, re, moved), jnp.where(lower, moved, im)


def own_rows(coil, got, fold, fold_t, pick, direction, residual, image):
    hbm = pl.BlockSpec(memory_space=pltpu.HBM)
    vmem = pl.BlockSpec(memory_space=pltpu.VMEM)
    return pl.pallas_call(
        own_rows_kernel,
        in_specs=[pl.BlockSpec(memory_space=pltpu.SMEM)] + [vmem] * 4 + [hbm] * 3,
        out_specs=[vmem] * 3,
        out_shape=[
            jax.ShapeDtypeStruct((2, 2, 512, 512), jnp.float32),
            jax.ShapeDtypeStruct((16, 16, 512), jnp.bfloat16),
            jax.ShapeDtypeStruct((3, 8, 32, 128), jnp.float32),
        ],
        scratch_shapes=[
            pltpu.VMEM((2, 2, 256, 512), jnp.bfloat16),
            pltpu.VMEM((2, 2, 256, 512), jnp.bfloat16),
            pltpu.VMEM((3, 2, 8, 32, 128), jnp.float32),
            pltpu.SemaphoreType.DMA((3,)),
        ],
        compiler_params=pltpu.CompilerParams(vmem_limit_bytes=16 * 1024 * 1024),
        name="own_rows",
    )(coil, got, fold, fold_t, pick, direction, residual, image)


def operator_kernel(
    coil_ref, got_ref, mate_ref, share_ref, mask_ref, fold_ref, fold_t_ref, pick_ref, pick_t_ref,
    z_back_ref, y_even_ref, y_odd_ref,
    keep_ref, send_ref,
    image_s, spec_s, even_s, odd_s, mask_t_s, mask_s,
):
    size = 512
    half = 256
    f32 = jnp.float32
    bf16 = jnp.bfloat16
    core = coil_ref[0] % 2
    mask_t_s[:, core] = mask_ref[...]
    mask_t_s[:, 1 - core] = mask_columns(mate_ref[:, pl.ds(32, 16), :], pick_ref)
    mask_s[...] = dot(pick_t_ref[...], mask_t_s[...].reshape(size, size)).T

    def store(coil, part, start, value):
        spec_s[coil, part, :, pl.ds(start, 128)] = value

    dir_parts = [mate_ref.at[:, pl.ds(part * 16, 16), :] for part in range(2)]
    spectrum_rows(got_ref, dir_parts, 1 - core, fold_ref, image_s, store)

    def sens(coil, part, block, lanes):
        rows = got_ref[pl.ds(block * 8, 8), pl.ds((part * 2 + coil) * 32, 32), lanes]
        return rows.reshape(half, -1).astype(f32)

    first_row = lax.broadcasted_iota(jnp.int32, (64, half), 0) == 0
    fulls = [
        [dot(fold_t_ref[1 - core], spec_s[coil, part]) for part in range(2)] for coil in range(2)
    ]
    for coil in range(2):
        full_re, full_im = fulls[coil]
        for nb in range(2):
            cols = pl.ds(nb * half, half)
            from_re = full_re[:, nb * half : nb * half + half] + share_ref[coil, 0, :, cols]
            from_im = full_im[:, nb * half : nb * half + half] + share_ref[coil, 1, :, cols]

            def kept(rest):
                pieces = [[], []]
                for side, at in enumerate(QUARTERS[rest]):
                    rows = slice(at * 64, at * 64 + 64)
                    rows_2 = slice(half + at * 64, half + at * 64 + 64)
                    re_cos, re_sin = from_re[rows], from_re[rows_2]
                    im_cos, im_sin = from_im[rows], from_im[rows_2]
                    if side == 0:
                        value, first = (re_cos + im_sin, im_cos - re_sin), (re_cos, im_cos)
                    else:
                        value, first = (re_cos - im_sin, im_cos + re_sin), (re_sin, im_sin)
                    keep = mask_s[rows_2 if side else rows, cols]
                    for part in range(2):
                        piece = jnp.where(first_row, first[part], value[part]) if at == 0 else value[part]
                        pieces[part].append((piece * keep).astype(bf16))
                return jnp.concatenate(pieces[0] + pieces[1], axis=0)

            e0, e1, e2, e3 = (dot(z_back_ref[rest], kept(rest)) for rest in range(4))
            sum_02, dif_02, sum_13, dif_13 = e0 + e2, e0 - e2, e1 + e3, e1 - e3
            turned = (dif_02[:128] - dif_13[128:], dif_02[128:] + dif_13[:128])
            turned_back = (dif_02[:128] + dif_13[128:], dif_02[128:] - dif_13[:128])
            plus, minus = sum_02 + sum_13, sum_02 - sum_13
            quarters = ((plus[:128], plus[128:]), turned, (minus[:128], minus[128:]), turned_back)
            for part in range(2):
                at = pl.ds(part * half + nb * 128, 128)
                for block in range(4):
                    back = quarters[block][part].astype(bf16)
                    even_s[coil, pl.ds(block * 128, 128), at] = back[:, :128]
                    odd_s[coil, pl.ds(block * 128, 128), at] = back[:, 128:]

    wholes = [
        [
            [dot(ref[coil, pl.ds(block * half, half), :], table[...]) for ref, table in ((even_s, y_even_ref), (odd_s, y_odd_ref))]
            for coil in range(2)
        ]
        for block in range(2)
    ]
    for block in range(2):
        sums = [[0.0, 0.0], [0.0, 0.0]]
        for coil in range(2):
            even, odd = wholes[block][coil]
            for yb in range(2):
                full = even + odd if yb == 0 else even - odd
                re, im = full[:, :half], full[:, half:]
                sens_re, sens_im = (sens(coil, part, block, pl.ds(yb * half, half)) for part in range(2))
                sums[yb][0] += sens_re * re + sens_im * im
                sums[yb][1] += sens_re * im - sens_im * re
        for yb in range(2):
            for lb in range(2):
                lanes = slice(lb * 128, lb * 128 + 128)
                even, odd = paired(sums[yb][0][:, lanes], sums[yb][1][:, lanes])
                slabs = pl.ds(block * 8, 8)
                keep_ref[slabs, yb * 2 + lb] = jnp.where(core == 0, even, odd).reshape(8, 32, 128)
                send_ref[slabs, yb * 2 + lb] = jnp.where(core == 0, odd, even).reshape(8, 32, 128).astype(bf16)


def operator(coil, got, mate, share, mask, fold_tabs):
    smem = pl.BlockSpec(memory_space=pltpu.SMEM)
    vmem = pl.BlockSpec(memory_space=pltpu.VMEM)
    return pl.pallas_call(
        operator_kernel,
        in_specs=[smem] + [vmem] * 11,
        out_specs=[vmem] * 2,
        out_shape=[
            jax.ShapeDtypeStruct((16, 4, 32, 128), jnp.float32),
            jax.ShapeDtypeStruct((16, 4, 32, 128), jnp.bfloat16),
        ],
        scratch_shapes=[
            pltpu.VMEM((2, 2, 256, 512), jnp.bfloat16),
            pltpu.VMEM((2, 2, 256, 512), jnp.bfloat16),
            pltpu.VMEM((2, 512, 512), jnp.bfloat16),
            pltpu.VMEM((2, 512, 512), jnp.bfloat16),
            pltpu.VMEM((16, 2, 16, 512), jnp.bfloat16),
            pltpu.VMEM((512, 512), jnp.float32),
        ],
        compiler_params=pltpu.CompilerParams(vmem_limit_bytes=32 * 1024 * 1024),
        name="operator",
    )(coil, got, mate, share, mask, *fold_tabs)


def sums_kernel(part_ref, own_ref, applied_ref, sums_ref):
    def body(x, carry):
        rr, da, ra, aa = carry
        total = jnp.zeros(applied_ref.shape[1:], jnp.float32)
        for coil in range(4):
            for pair in range(2):
                total += part_ref[x, pair, coil].astype(jnp.float32)
        direction = own_ref[0, x]
        residual = own_ref[1, x]
        applied = total + ridge_weight * direction
        applied_ref[x] = applied
        return (
            rr + residual * residual,
            da + direction * applied,
            ra + residual * applied,
            aa + applied * applied,
        )

    zero = jnp.zeros(applied_ref.shape[1:], jnp.float32)
    sums = lax.fori_loop(0, applied_ref.shape[0], body, (zero,) * 4)
    lane = lax.broadcasted_iota(jnp.int32, (1, 128), 1)
    row = jnp.zeros((1, 128), jnp.float32)
    for index, value in enumerate(sums):
        row = jnp.where(lane == index, jnp.sum(value), row)
    sums_ref[...] = jnp.broadcast_to(row, sums_ref.shape)


def final_kernel(all_ref, applied_ref, own_ref, img_out, res_out, dir_out):
    total = jnp.sum(all_ref[...], axis=0, keepdims=True)
    rr, da, ra, aa = (total[:, i : i + 1] for i in range(4))
    step = rr / da
    new = rr + step * (step * aa - 2.0 * ra)
    beta = new / rr
    step = step.reshape(1, 1, 1)
    beta = beta.reshape(1, 1, 1)
    direction = own_ref[0]
    img = own_ref[2] + step * direction
    res = own_ref[1] - step * applied_ref[...]
    nxt = res + beta * direction
    for out, value in ((img_out, img), (res_out, res), (dir_out, nxt)):
        out[0] = value[:, :, :64]
        out[1] = value[:, :, 64:]


def on_device(image, residual, direction, sensitivity, sampling):
    fold_tabs = [jnp.asarray(table) for table in fold_tables(512)]
    coil = lax.axis_index("coil").reshape(1)
    mates = [(at, at ^ 1) for at in range(8)]
    same_core = [[at * 16 + to for to in range(16) for at in range(side, 8, 2)] for side in range(2)]
    packed = pack(coil % 2, sensitivity, direction, sampling.T)
    got = lax.all_to_all(packed.reshape(16, 176, 512), "space", 0, 0, tiled=True)
    mate = lax.ppermute(got[:, 128:], "coil", mates)
    share, mask, own = own_rows(coil, got, *fold_tabs[:3], direction, residual, image)
    keep, send = operator(coil, got, mate, share, mask, fold_tabs)
    pair_sum = (keep + lax.ppermute(send, "coil", mates)).astype(jnp.bfloat16)
    parts = lax.all_to_all(
        pair_sum.reshape(64, 32, 128), ("coil", "space"), 0, 0, axis_index_groups=same_core, tiled=True
    )
    whole = pl.BlockSpec(memory_space=pltpu.VMEM)
    params = pltpu.CompilerParams(vmem_limit_bytes=vmem_limit)
    applied, sums = pl.pallas_call(
        sums_kernel,
        in_specs=[whole] * 2,
        out_specs=[whole] * 2,
        out_shape=[
            jax.ShapeDtypeStruct((8, 32, 128), jnp.float32),
            jax.ShapeDtypeStruct((128, 128), jnp.float32),
        ],
        compiler_params=params,
        name="sums",
    )(parts.reshape(8, 2, 4, 32, 128), own)
    everyone = lax.all_to_all(sums, ("space", "coil"), split_axis=0, concat_axis=0, tiled=True)
    outs = pl.pallas_call(
        final_kernel,
        in_specs=[whole] * 3,
        out_specs=[whole] * 3,
        out_shape=[jax.ShapeDtypeStruct((2, 8, 32, 64), jnp.float32)] * 3,
        compiler_params=params,
        name="final",
    )(everyone, applied, own)
    return tuple(outs)


def solution(mesh):
    placed = (
        P(None, None, "space", None),
        P(None, None, "space", None),
        P(None, None, "space", None),
        P(None, "coil", None, "space", None),
        P(None, "space"),
    )
    return jax.shard_map(
        on_device,
        mesh=mesh,
        in_specs=placed,
        out_specs=(P(None, None, "space", "coil"),) * 3,
        check_vma=False,
    )
```

```python
import math

import jax
import jax.numpy as jnp
import ml_dtypes
import numpy as np
from jax import lax
from jax.experimental import pallas as pl
from jax.experimental.pallas import tpu as pltpu
from jax.sharding import PartitionSpec as P

ridge_weight = 0.1
vmem_limit = 8 * 1024 * 1024


def tables(length):
    counter = np.arange(length, dtype=np.int32)
    product_mod = counter[:, None] * counter[None, :] % length
    phase_angle = product_mod.astype(np.float32) * np.float32(2.0 * math.pi / length)
    norm_scale = np.float32(1.0 / math.sqrt(length))
    return np.cos(phase_angle) * norm_scale, np.sin(phase_angle) * norm_scale


QUARTERS = ((0, 0), (2, 3), (1, 1), (3, 2))


def fold_tables(length):
    cos_t, sin_t = tables(length)
    half = length // 2
    low = np.concatenate([np.arange(rest, half, 4) for rest in (0, 2, 1, 3)])
    high = np.where(low == 0, half, length - low)
    sine = sin_t[:, low].copy()
    sine[:, 0] = cos_t[:, half]
    fold = np.concatenate([cos_t[:, low], sine], axis=1)
    pick = np.eye(length, dtype=np.float32)[:, np.concatenate([low, high])]

    def inverse(rows, at):
        cos_g, sin_g = cos_t[:rows, at], sin_t[:rows, at]
        return np.block([[cos_g, -sin_g], [sin_g, cos_g]])

    quarter = half // 4
    by_core = fold.T.reshape(length, 16, 2, 16).transpose(2, 0, 1, 3).reshape(2, length, half)
    outs = [fold, by_core, pick, pick.T]
    outs.append(
        np.stack(
            [
                inverse(half // 2, np.concatenate([low[a * quarter :][:quarter], high[b * quarter :][:quarter]]))
                for a, b in QUARTERS
            ]
        )
    )
    for start in (0, half // 2):
        group = slice(start, start + half // 2)
        outs.append(inverse(half, np.concatenate([low[group], high[group]])).T)
    return [np.ascontiguousarray(out).astype(ml_dtypes.bfloat16) for out in outs]


def pack_kernel(core_ref, sens_ref, dir_ref, mask_ref, out_ref, sens_s, dir_s, mask_s, small_s, in_sems, out_sems):
    core_rows = pl.ds(pl.multiple_of(core_ref[0] * 16, 16), 16)
    small = [
        pltpu.make_async_copy(dir_ref.at[part, :, core_rows, :], dir_s.at[part], in_sems.at[8 + part])
        for part in range(2)
    ]
    small.append(pltpu.make_async_copy(mask_ref.at[core_rows, :], mask_s, in_sems.at[10]))
    pairs = [(part, coil) for part in range(2) for coil in range(4)]
    loads = [
        pltpu.make_async_copy(sens_ref.at[part, coil], sens_s.at[part, coil], in_sems.at[part * 4 + coil])
        for part, coil in pairs
    ]
    stores = [
        pltpu.make_async_copy(
            sens_s.at[part, coil],
            out_ref.at[:, coil // 2, pl.ds((part * 2 + coil % 2) * 32, 32), :],
            out_sems.at[part * 4 + coil],
        )
        for part, coil in pairs
    ]
    stores += [
        pltpu.make_async_copy(small_s, out_ref.at[:, half, pl.ds(128, 48), :], out_sems.at[8 + half])
        for half in range(2)
    ]
    for copy in small + loads:
        copy.start()
    for copy in small:
        copy.wait()
    kept = mask_s[...].astype(jnp.bfloat16)
    for x in range(8):
        for part in range(2):
            small_s[x, pl.ds(part * 16, 16), :] = dir_s[part, x].astype(jnp.bfloat16)
        small_s[x, pl.ds(32, 16), :] = kept
    for copy in stores[8:]:
        copy.start()
    for load, store in zip(loads, stores):
        load.wait()
        store.start()
    for copy in stores:
        copy.wait()


def pack(core, sensitivity, direction, mask_t):
    hbm = pl.BlockSpec(memory_space=pltpu.HBM)
    return pl.pallas_call(
        pack_kernel,
        in_specs=[pl.BlockSpec(memory_space=pltpu.SMEM), hbm, hbm, hbm],
        out_specs=hbm,
        out_shape=jax.ShapeDtypeStruct((8, 2, 176, 512), jnp.bfloat16),
        scratch_shapes=[
            pltpu.VMEM((2, 4, 8, 32, 512), jnp.bfloat16),
            pltpu.VMEM((2, 8, 16, 512), jnp.float32),
            pltpu.VMEM((16, 512), jnp.int32),
            pltpu.VMEM((8, 48, 512), jnp.bfloat16),
            pltpu.SemaphoreType.DMA((11,)),
            pltpu.SemaphoreType.DMA((10,)),
        ],
        compiler_params=pltpu.CompilerParams(vmem_limit_bytes=60 * 1024 * 1024),
        name="pack",
    )(core, sensitivity, direction, mask_t)


def dot(left, right):
    return jnp.dot(left, right, preferred_element_type=jnp.float32)


def spectrum_rows(got_ref, dir_parts, core, fold_ref, image_s, store):
    half = 256
    first_lane = lax.broadcasted_iota(jnp.int32, (half, 128), 1) == 0
    for coil in range(2):
        for yb in range(2):
            cols = pl.ds(yb * half, half)
            dir_re, dir_im = (part[:, :, cols].reshape(half, half).astype(jnp.float32) for part in dir_parts)
            sens_re, sens_im = (
                got_ref[:, pl.ds(pl.multiple_of((part * 2 + coil) * 32 + core * 16, 16), 16), cols]
                .reshape(half, half)
                .astype(jnp.float32)
                for part in range(2)
            )
            image_s[coil, 0, :, cols] = (sens_re * dir_re - sens_im * dir_im).astype(jnp.bfloat16)
            image_s[coil, 1, :, cols] = (sens_re * dir_im + sens_im * dir_re).astype(jnp.bfloat16)
    for coil in range(2):
        from_re = dot(image_s[coil, 0], fold_ref[...])
        from_im = dot(image_s[coil, 1], fold_ref[...])
        re_cos, re_sin = from_re[:, :half], from_re[:, half:]
        im_cos, im_sin = from_im[:, :half], from_im[:, half:]
        low = (re_cos + im_sin, im_cos - re_sin)
        high = (re_cos - im_sin, im_cos + re_sin)
        low_first = (re_cos, im_cos)
        high_first = (re_sin, im_sin)
        for part in range(2):
            for start, value, first in ((0, low[part], low_first[part]), (half, high[part], high_first[part])):
                edge = jnp.where(first_lane, first[:, :128], value[:, :128])
                store(coil, part, start, edge.astype(jnp.bfloat16))
                store(coil, part, start + 128, value[:, 128:].astype(jnp.bfloat16))


def own_rows_kernel(
    coil_ref, got_ref, fold_ref, fold_t_ref, pick_ref, dir_ref, res_ref, img_ref,
    share_ref, mask_ref, own_ref,
    image_s, spec_s, own_s, sems,
):
    core = coil_ref[0] % 2
    own_lanes = pl.ds(pl.multiple_of(coil_ref[0] // 2 * 128, 128), 128)
    own_copies = [
        pltpu.make_async_copy(ref.at[:, :, :, own_lanes], own_s.at[index], sems.at[index])
        for index, ref in enumerate((dir_ref, res_ref, img_ref))
    ]
    for copy in own_copies:
        copy.start()

    def store(coil, part, start, value):
        spec_s[coil, part, :, pl.ds(start, 128)] = value

    mask_ref[...] = mask_columns(got_ref[:, pl.ds(160, 16), :], pick_ref)
    dir_parts = [got_ref.at[:, pl.ds(128 + part * 16, 16), :] for part in range(2)]
    spectrum_rows(got_ref, dir_parts, core, fold_ref, image_s, store)
    for coil in range(2):
        for part in range(2):
            share_ref[coil, part] = dot(fold_t_ref[core], spec_s[coil, part])
    for copy in own_copies:
        copy.wait()
    for index in range(3):
        even, odd = paired(*(own_s[index, part].reshape(256, 128) for part in range(2)))
        own_ref[index] = jnp.where(core == 0, even, odd).reshape(8, 32, 128)


def mask_columns(rows, pick_ref):
    return dot(rows.reshape(256, 512), pick_ref[...]).astype(jnp.bfloat16).reshape(16, 16, 512)


def paired(re, im):
    lower = lax.broadcasted_iota(jnp.int32, re.shape, 1) < 64
    moved = pltpu.roll(jnp.where(lower, im, re), 64, 1)
    return jnp.where(lower, re, moved), jnp.where(lower, moved, im)


def own_rows(coil, got, fold, fold_t, pick, direction, residual, image):
    hbm = pl.BlockSpec(memory_space=pltpu.HBM)
    vmem = pl.BlockSpec(memory_space=pltpu.VMEM)
    return pl.pallas_call(
        own_rows_kernel,
        in_specs=[pl.BlockSpec(memory_space=pltpu.SMEM)] + [vmem] * 4 + [hbm] * 3,
        out_specs=[vmem] * 3,
        out_shape=[
            jax.ShapeDtypeStruct((2, 2, 512, 512), jnp.float32),
            jax.ShapeDtypeStruct((16, 16, 512), jnp.bfloat16),
            jax.ShapeDtypeStruct((3, 8, 32, 128), jnp.float32),
        ],
        scratch_shapes=[
            pltpu.VMEM((2, 2, 256, 512), jnp.bfloat16),
            pltpu.VMEM((2, 2, 256, 512), jnp.bfloat16),
            pltpu.VMEM((3, 2, 8, 32, 128), jnp.float32),
            pltpu.SemaphoreType.DMA((3,)),
        ],
        compiler_params=pltpu.CompilerParams(vmem_limit_bytes=16 * 1024 * 1024),
        name="own_rows",
    )(coil, got, fold, fold_t, pick, direction, residual, image)


def operator_kernel(
    coil_ref, got_ref, mate_ref, share_ref, mask_ref, fold_ref, fold_t_ref, pick_ref, pick_t_ref,
    z_back_ref, y_even_ref, y_odd_ref,
    keep_ref, send_ref,
    image_s, spec_s, even_s, odd_s, mask_t_s, mask_s,
):
    size = 512
    half = 256
    f32 = jnp.float32
    bf16 = jnp.bfloat16
    core = coil_ref[0] % 2
    mask_t_s[:, core] = mask_ref[...]
    mask_t_s[:, 1 - core] = mask_columns(mate_ref[:, pl.ds(32, 16), :], pick_ref)
    mask_s[...] = dot(pick_t_ref[...], mask_t_s[...].reshape(size, size)).T

    def store(coil, part, start, value):
        spec_s[coil, part, :, pl.ds(start, 128)] = value

    dir_parts = [mate_ref.at[:, pl.ds(part * 16, 16), :] for part in range(2)]
    spectrum_rows(got_ref, dir_parts, 1 - core, fold_ref, image_s, store)

    def sens(coil, part, block, lanes):
        rows = got_ref[pl.ds(block * 8, 8), pl.ds((part * 2 + coil) * 32, 32), lanes]
        return rows.reshape(half, -1).astype(f32)

    first_row = lax.broadcasted_iota(jnp.int32, (64, half), 0) == 0
    fulls = [
        [dot(fold_t_ref[1 - core], spec_s[coil, part]) for part in range(2)] for coil in range(2)
    ]
    for coil in range(2):
        full_re, full_im = fulls[coil]
        for nb in range(2):
            cols = pl.ds(nb * half, half)
            from_re = full_re[:, nb * half : nb * half + half] + share_ref[coil, 0, :, cols]
            from_im = full_im[:, nb * half : nb * half + half] + share_ref[coil, 1, :, cols]

            def kept(rest):
                pieces = [[], []]
                for side, at in enumerate(QUARTERS[rest]):
                    rows = slice(at * 64, at * 64 + 64)
                    rows_2 = slice(half + at * 64, half + at * 64 + 64)
                    re_cos, re_sin = from_re[rows], from_re[rows_2]
                    im_cos, im_sin = from_im[rows], from_im[rows_2]
                    if side == 0:
                        value, first = (re_cos + im_sin, im_cos - re_sin), (re_cos, im_cos)
                    else:
                        value, first = (re_cos - im_sin, im_cos + re_sin), (re_sin, im_sin)
                    keep = mask_s[rows_2 if side else rows, cols]
                    for part in range(2):
                        piece = jnp.where(first_row, first[part], value[part]) if at == 0 else value[part]
                        pieces[part].append((piece * keep).astype(bf16))
                return jnp.concatenate(pieces[0] + pieces[1], axis=0)

            e0, e1, e2, e3 = (dot(z_back_ref[rest], kept(rest)) for rest in range(4))
            sum_02, dif_02, sum_13, dif_13 = e0 + e2, e0 - e2, e1 + e3, e1 - e3
            turned = (dif_02[:128] - dif_13[128:], dif_02[128:] + dif_13[:128])
            turned_back = (dif_02[:128] + dif_13[128:], dif_02[128:] - dif_13[:128])
            plus, minus = sum_02 + sum_13, sum_02 - sum_13
            quarters = ((plus[:128], plus[128:]), turned, (minus[:128], minus[128:]), turned_back)
            for part in range(2):
                at = pl.ds(part * half + nb * 128, 128)
                for block in range(4):
                    back = quarters[block][part].astype(bf16)
                    even_s[coil, pl.ds(block * 128, 128), at] = back[:, :128]
                    odd_s[coil, pl.ds(block * 128, 128), at] = back[:, 128:]

    wholes = [
        [
            [dot(ref[coil, pl.ds(block * half, half), :], table[...]) for ref, table in ((even_s, y_even_ref), (odd_s, y_odd_ref))]
            for coil in range(2)
        ]
        for block in range(2)
    ]
    for block in range(2):
        sums = [[0.0, 0.0], [0.0, 0.0]]
        for coil in range(2):
            even, odd = wholes[block][coil]
            for yb in range(2):
                full = even + odd if yb == 0 else even - odd
                re, im = full[:, :half], full[:, half:]
                sens_re, sens_im = (sens(coil, part, block, pl.ds(yb * half, half)) for part in range(2))
                sums[yb][0] += sens_re * re + sens_im * im
                sums[yb][1] += sens_re * im - sens_im * re
        for yb in range(2):
            for lb in range(2):
                lanes = slice(lb * 128, lb * 128 + 128)
                even, odd = paired(sums[yb][0][:, lanes], sums[yb][1][:, lanes])
                slabs = pl.ds(block * 8, 8)
                keep_ref[slabs, yb * 2 + lb] = jnp.where(core == 0, even, odd).reshape(8, 32, 128)
                send_ref[slabs, yb * 2 + lb] = jnp.where(core == 0, odd, even).reshape(8, 32, 128).astype(bf16)


def operator(coil, got, mate, share, mask, fold_tabs):
    smem = pl.BlockSpec(memory_space=pltpu.SMEM)
    vmem = pl.BlockSpec(memory_space=pltpu.VMEM)
    return pl.pallas_call(
        operator_kernel,
        in_specs=[smem] + [vmem] * 11,
        out_specs=[vmem] * 2,
        out_shape=[
            jax.ShapeDtypeStruct((16, 4, 32, 128), jnp.float32),
            jax.ShapeDtypeStruct((16, 4, 32, 128), jnp.bfloat16),
        ],
        scratch_shapes=[
            pltpu.VMEM((2, 2, 256, 512), jnp.bfloat16),
            pltpu.VMEM((2, 2, 256, 512), jnp.bfloat16),
            pltpu.VMEM((2, 512, 512), jnp.bfloat16),
            pltpu.VMEM((2, 512, 512), jnp.bfloat16),
            pltpu.VMEM((16, 2, 16, 512), jnp.bfloat16),
            pltpu.VMEM((512, 512), jnp.float32),
        ],
        compiler_params=pltpu.CompilerParams(vmem_limit_bytes=32 * 1024 * 1024),
        name="operator",
    )(coil, got, mate, share, mask, *fold_tabs)


def sums_kernel(part_ref, own_ref, applied_ref, sums_ref):
    def body(x, carry):
        rr, da, ra, aa = carry
        total = jnp.zeros(applied_ref.shape[1:], jnp.float32)
        for coil in range(4):
            for pair in range(2):
                total += part_ref[x, pair, coil].astype(jnp.float32)
        direction = own_ref[0, x]
        residual = own_ref[1, x]
        applied = total + ridge_weight * direction
        applied_ref[x] = applied
        return (
            rr + residual * residual,
            da + direction * applied,
            ra + residual * applied,
            aa + applied * applied,
        )

    zero = jnp.zeros(applied_ref.shape[1:], jnp.float32)
    sums = lax.fori_loop(0, applied_ref.shape[0], body, (zero,) * 4)
    lane = lax.broadcasted_iota(jnp.int32, (1, 128), 1)
    row = jnp.zeros((1, 128), jnp.float32)
    for index, value in enumerate(sums):
        row = jnp.where(lane == index, jnp.sum(value), row)
    sums_ref[...] = jnp.broadcast_to(row, sums_ref.shape)


def final_kernel(all_ref, applied_ref, own_ref, img_out, res_out, dir_out):
    total = jnp.sum(all_ref[...], axis=0, keepdims=True)
    rr, da, ra, aa = (total[:, i : i + 1] for i in range(4))
    step = rr / da
    new = rr + step * (step * aa - 2.0 * ra)
    beta = new / rr
    step = step.reshape(1, 1, 1)
    beta = beta.reshape(1, 1, 1)
    direction = own_ref[0]
    img = own_ref[2] + step * direction
    res = own_ref[1] - step * applied_ref[...]
    nxt = res + beta * direction
    for out, value in ((img_out, img), (res_out, res), (dir_out, nxt)):
        out[0] = value[:, :, :64]
        out[1] = value[:, :, 64:]


def on_device(image, residual, direction, sensitivity, sampling):
    fold_tabs = [jnp.asarray(table) for table in fold_tables(512)]
    coil = lax.axis_index("coil").reshape(1)
    mates = [(at, at ^ 1) for at in range(8)]
    same_core = [[at * 16 + to for to in range(16) for at in range(side, 8, 2)] for side in range(2)]
    packed = pack(coil % 2, sensitivity, direction, sampling.T)
    got = lax.all_to_all(packed.reshape(16, 176, 512), "space", 0, 0, tiled=True)
    mate = lax.ppermute(got[:, 128:], "coil", mates)
    share, mask, own = own_rows(coil, got, *fold_tabs[:3], direction, residual, image)
    keep, send = operator(coil, got, mate, share, mask, fold_tabs)
    pair_sum = (keep + lax.ppermute(send, "coil", mates)).astype(jnp.bfloat16)
    parts = lax.all_to_all(
        pair_sum.reshape(64, 32, 128), ("coil", "space"), 0, 0, axis_index_groups=same_core, tiled=True
    )
    whole = pl.BlockSpec(memory_space=pltpu.VMEM)
    params = pltpu.CompilerParams(vmem_limit_bytes=vmem_limit)
    applied, sums = pl.pallas_call(
        sums_kernel,
        in_specs=[whole] * 2,
        out_specs=[whole] * 2,
        out_shape=[
            jax.ShapeDtypeStruct((8, 32, 128), jnp.float32),
            jax.ShapeDtypeStruct((128, 128), jnp.float32),
        ],
        compiler_params=params,
        name="sums",
    )(parts.reshape(8, 2, 4, 32, 128), own)
    everyone = lax.all_to_all(sums, ("space", "coil"), split_axis=0, concat_axis=0, tiled=True)
    outs = pl.pallas_call(
        final_kernel,
        in_specs=[whole] * 3,
        out_specs=[whole] * 3,
        out_shape=[jax.ShapeDtypeStruct((2, 8, 32, 64), jnp.float32)] * 3,
        compiler_params=params,
        name="final",
    )(everyone, applied, own)
    return tuple(outs)


def solution(mesh):
    placed = (
        P(None, None, "space", None),
        P(None, None, "space", None),
        P(None, None, "space", None),
        P(None, "coil", None, "space", None),
        P(None, "space"),
    )
    return jax.shard_map(
        on_device,
        mesh=mesh,
        in_specs=placed,
        out_specs=(P(None, None, "space", "coil"),) * 3,
        check_vma=False,
    )
```
